256 devices in a mesh: ctx: 8 (over z), exp: 8 (over y, x_lo), req: 4 (over x_hi, core).
Axes of the slice: x: 4 (x_hi: 2, x_lo: 2; x = x_hi * 2 + x_lo), y: 4, z: 8, core: 2. Of those that a mesh axis runs over, the one named last changes fastest.
Arguments:
- queries: bfloat16 [64, 2, 128, 576], P('req', None, ('ctx', 'exp')), parts along dimension 0, may hold values from -21 to 21
- latent_cache: bfloat16 [64, 32768, 576], P('req', ('ctx', 'exp')), parts along dimension 0, may hold values from -4 to 4
- context_lengths: int32 [64], P('req'), parts along dimension 0, may hold values from 16 to 32767, as said below
- value_up: bfloat16 [128, 512, 128], P(('ctx', 'exp')), may hold values from -0.25 to 0.25
- out_proj: bfloat16 [16384, 7168], P(('ctx', 'exp')), may hold values from -0.09375 to 0.09375
- residual: bfloat16 [128, 7168], P(('req', 'exp')), parts along dimension 0, may hold values from -3 to 3
- norm_gain: bfloat16 [7168], replicated, may hold values from 0.099609375 to 1.8984375
- router: bfloat16 [7168, 8], replicated, may hold values from -0.125 to 0.125
- routes: int32 [128, 2], P(('req', 'exp')), parts along dimension 0, may hold values from 0 to 7, all different within a row; in each aligned block of 4 rows (0 to 3, 4 to 7, ...) at most 2 rows name the same one
- expert_gate: bfloat16 [8, 7168, 1024], P('exp', None, 'ctx'), may hold values from -0.0625 to 0.0625
- expert_up: bfloat16 [8, 7168, 1024], P('exp', None, 'ctx'), may hold values from -0.0625 to 0.0625
- expert_down: bfloat16 [8, 1024, 7168], P('exp', 'ctx'), may hold values from -0.375 to 0.375
Outputs:
- output: bfloat16 [128, 7168], P(('req', 'exp'), 'ctx'), parts along dimension 0
The draws below stay inside these ranges and needn't reach their ends.
There are 4 independent parts, one for each index of `req`. The reference program is written for one: setup_inputs(seed, part) draws one part's arguments, and reference() takes and returns one part's arrays. A program takes and returns all parts, laid end to end along the dimension named above; an argument that names none is the same for every part. Nothing has to cross between parts.
Inputs may be any that keep to these rules, and one draw needn't show every extreme that they name: Verify row j of request r sees context positions below context_lengths[r] + j; in every draw one request has 32767. `routes`: each row names 2 different experts; in each aligned block of 4 rows (the rows of one index of exp) no expert is named by more than 2 rows.
All inputs are finite; a program needn't handle non-finite values.
Results may differ from the reference program's by a relative error of at most 0.028.
Values may be sent and summed in bfloat16 or wider, within the bound.
No kernel may reach another device: no remote copies, remote signals or barrier semaphores. Data moves between devices by JAX's collectives and lax.ppermute only.
A program may use at most 128 MiB of HBM per device.

```python
import math
import jax
import jax.numpy as jnp
import numpy as np
from jax import lax

D = 7168
HEADS = 128
LAT = 512
ROPE = 64
VDIM = 128
FF = 1024
TOP = 2
REQS = 16
CTX = 32768
ROWS = 32
ROW_DEV = 4
EXPERTS = 8
CAP = 2


def cache_values(key, width):
    normal_part = jnp.clip(jax.random.normal(key, (REQS, CTX, LAT + ROPE), jnp.float32), -4.0, 4.0)
    flat_part = jax.random.uniform(key, (REQS, CTX, LAT + ROPE), jnp.float32, minval=-1.7, maxval=1.7)
    return jnp.where(width > 0.0, flat_part, normal_part)


def draw_latent_cache(key, part):
    values = cache_values(key, 0.0)
    return values.astype(jnp.bfloat16)


def draw_queries(key, part):
    key = jax.random.fold_in(key, 2)
    values = jnp.clip(jax.random.normal(key, (REQS, 2, HEADS, LAT + ROPE), jnp.float32), -4.0, 4.0)
    return values.astype(jnp.bfloat16)


def draw_context_lengths(key, part):
    key = jax.random.fold_in(key, 3)
    lengths = jax.random.randint(key, (REQS,), 16, CTX)
    longest = jax.random.randint(jax.random.fold_in(key, 4), (), 0, REQS)
    return jnp.where(jnp.arange(REQS) == longest, CTX - 1, lengths).astype(jnp.int32)


def shard_levels(stream_key, shape, split, low, high):
    gain = 1.0
    for position, blocks in split:
        heights = jax.random.uniform(jax.random.fold_in(jax.random.fold_in(stream_key, 6), position), (blocks,), jnp.float32, low / len(split), high / len(split))
        gain = gain * jnp.repeat(jnp.exp(heights), shape[position] // blocks).reshape((-1,) + (1,) * (len(shape) - 1 - position))
    return gain


def routed_block(rng, own, number, rows, number_of, top, limit, lean):
    ranking = jax.random.permutation(rng, number_of)
    crowded, usual = load_shares(number_of, rows * top, limit, lean, True), load_shares(number_of, rows * top, limit, lean, False)
    places = jnp.arange(number_of)

    def named(sizes, offset_by):
        used = int((sizes > 0).sum())
        fixed = max(1, used // 4)
        moved = fixed + (places - fixed + offset_by * (used - fixed)) % max(1, number_of - fixed)
        return jnp.zeros((number_of,), jnp.int32).at[ranking[jnp.where(places < fixed, places, moved)]].set(jnp.asarray(sizes, jnp.int32))

    sizes = jnp.where(number % 4 == 0, named(crowded, number // 4), named(usual, number - number // 4 - 1))
    mixed = jax.random.permutation(jax.random.fold_in(own, 3), number_of)
    giver, taker = mixed[0:number_of // 2 * 2:2], mixed[1:number_of // 2 * 2:2]
    room = jnp.minimum(sizes[giver] - 1, limit - sizes[taker]) // 2
    room = jnp.where((giver == ranking[0]) | (taker == ranking[0]) | (sizes[taker] == 0), 0, jnp.maximum(room, 0))
    moved = jax.random.randint(jax.random.fold_in(own, 4), (number_of // 2,), 0, 1 << 20) % (room + 1)
    sizes = sizes.at[giver].add(-moved).at[taker].add(moved)
    items = jnp.searchsorted(jnp.cumsum(sizes), jnp.arange(rows * top), side="right").astype(jnp.int32)
    listing = items.reshape(top, rows).T
    listing = listing[jax.random.permutation(jax.random.fold_in(own, 1), rows)]
    offset_by = jax.random.randint(jax.random.fold_in(own, 2), (rows, 1), 0, top)
    return jnp.take_along_axis(listing, (jnp.arange(top)[None, :] + offset_by) % top, axis=1)


def load_shares(number_of, total, most, lean, full):
    loads = [(1 << 20) // math.isqrt(standing ** lean) + 1 for standing in range(1, number_of + 1)]
    largest = most if full else min(most, max(-(-total // number_of), total * loads[0] // sum(loads)))
    least = 1 if total - largest >= number_of - 1 else 0
    holding, rest = [largest] + [least] * (number_of - 1), total - largest - least * (number_of - 1)
    while rest > 0:
        free = [i for i in range(1, number_of) if holding[i] < largest] or [i for i in range(1, number_of) if holding[i] < most]
        whole, remaining = sum([loads[i] for i in free]), rest
        for i in free:
            more = min(most - holding[i], max(1, remaining * loads[i] // whole), rest)
            holding[i] = holding[i] + more
            rest = rest - more
    return np.array(holding)


def centred(rng, dims, spread, reach, cuts=(), kind=jnp.bfloat16):
    level = shard_levels(rng, dims, cuts, -0.22, 0.18) if cuts else 1.0
    drawn = jax.random.normal(rng, dims, jnp.float32) * spread * level
    return jnp.minimum(jnp.maximum(drawn, -reach), reach).astype(kind)


def setup_inputs(seed: int = 0, part: int = 0) -> dict:
    key_of = jax.random.split(jax.random.key(seed), 13)
    part_keys = jax.random.split(jax.random.fold_in(key_of[12], part), 13)
    queries = draw_queries(jax.random.fold_in(jax.random.fold_in(key_of[12], part), 71), part)
    latent_cache = draw_latent_cache(jax.random.fold_in(jax.random.fold_in(key_of[12], part), 71), part)
    context_lengths = draw_context_lengths(jax.random.fold_in(jax.random.fold_in(key_of[12], part), 71), part)
    value_up = centred(key_of[3], (HEADS, LAT, VDIM), LAT ** -0.5, 0.25, ((0, 64),))
    out_proj = centred(key_of[4], (HEADS * VDIM, D), (HEADS * VDIM // 4) ** -0.5, 0.09375, ((0, 64),))
    residual = centred(part_keys[5], (ROWS, D), 0.5, 3.0, ((0, 8),))
    norm_gain = jnp.clip(1.0 + 0.18 * jax.random.normal(key_of[6], (D,), jnp.float32), 0.099609375, 1.8984375).astype(jnp.bfloat16)
    router = centred(key_of[7], (D, EXPERTS), (D // 4) ** -0.5, 0.125)
    routes_keys = jax.random.split(jax.random.fold_in(part_keys[8], 1), ROWS // ROW_DEV)
    routes_turns = jax.random.permutation(jax.random.fold_in(part_keys[8], 3), ROWS // ROW_DEV)
    routes = jax.vmap(lambda own, number: routed_block(jax.random.fold_in(part_keys[8], 2), own, number, ROW_DEV, EXPERTS, TOP, CAP, 2))(routes_keys, routes_turns).reshape((ROWS, TOP))
    expert_gate = centred(key_of[9], (EXPERTS, D, FF), D ** -0.5, 0.0625, ((0, 8), (2, 8)))
    expert_up = centred(key_of[10], (EXPERTS, D, FF), D ** -0.5, 0.0625, ((0, 8), (2, 8)))
    expert_down = centred(key_of[11], (EXPERTS, FF, D), (FF // 4) ** -0.5, 0.375, ((0, 8), (1, 8)))
    return dict(queries=queries, latent_cache=latent_cache, context_lengths=context_lengths, value_up=value_up, out_proj=out_proj, residual=residual, norm_gain=norm_gain, router=router, routes=routes, expert_gate=expert_gate, expert_up=expert_up, expert_down=expert_down)


route_scale = 2.5

def reference(queries, latent_cache, context_lengths, value_up, out_proj, residual, norm_gain, router, routes, expert_gate, expert_up, expert_down):
    score_scale = 1.0 / math.sqrt(VDIM + ROPE)
    positions = jnp.arange(CTX, dtype=jnp.int32)
    offsets = jnp.arange(2, dtype=jnp.int32)

    def attend(inputs):
        query_rows, cache_rows, length = inputs
        scores = jnp.einsum('jhd,td->jht', query_rows.astype(jnp.float32), cache_rows.astype(jnp.float32)) * score_scale
        visible = positions[None, None, :] < (length + offsets)[:, None, None]
        masked = jnp.where(visible, scores, -1e+30)
        row_max = lax.optimization_barrier(jnp.max(masked, axis=-1, keepdims=True))
        weights = jnp.where(visible, jnp.exp(masked - row_max), 0.0)
        weight_sum = lax.optimization_barrier(jnp.sum(weights, axis=-1))
        rounded = lax.optimization_barrier(weights.astype(jnp.bfloat16)).astype(jnp.float32)
        latents = cache_rows[:, :LAT].astype(jnp.float32)
        weighted = jnp.einsum('jht,tl->jhl', rounded, latents)
        return (weighted / weight_sum[..., None]).astype(jnp.bfloat16)
    context = lax.map(attend, (queries, latent_cache, context_lengths))
    head_out = jnp.einsum('rjhl,hlv->rjhv', context.astype(jnp.float32), value_up.astype(jnp.float32)).astype(jnp.bfloat16)
    head_out = head_out.reshape(ROWS, HEADS * VDIM)
    attention = jnp.dot(head_out, out_proj, preferred_element_type=jnp.float32)
    hidden = (residual.astype(jnp.float32) + attention).astype(jnp.bfloat16)
    hidden_wide = hidden.astype(jnp.float32)
    inverse = lax.rsqrt(lax.optimization_barrier(jnp.mean(hidden_wide * hidden_wide, axis=-1, keepdims=True)) + 1e-06)
    normed = (hidden_wide * inverse * norm_gain.astype(jnp.float32)).astype(jnp.bfloat16)
    affinity = jax.nn.sigmoid(jnp.dot(normed, router, preferred_element_type=jnp.float32))
    chosen = (routes[:, :, None] == jnp.arange(EXPERTS, dtype=jnp.int32)[None, None, :]).astype(jnp.float32)
    picked = lax.optimization_barrier(jnp.sum(chosen * affinity[:, None, :], axis=-1))
    gate_weights = route_scale * picked / lax.optimization_barrier(jnp.sum(picked, axis=-1, keepdims=True))
    mixing = lax.optimization_barrier(jnp.sum(gate_weights[:, :, None] * chosen, axis=1))

    def expert(expert_id):
        gate_part = jnp.dot(normed, expert_gate[expert_id], preferred_element_type=jnp.float32)
        up_part = jnp.dot(normed, expert_up[expert_id], preferred_element_type=jnp.float32)
        active = (jax.nn.silu(gate_part) * up_part).astype(jnp.bfloat16)
        return jnp.dot(active, expert_down[expert_id], preferred_element_type=jnp.float32)
    expert_rows = lax.map(expert, jnp.arange(EXPERTS, dtype=jnp.int32))
    mixture = jnp.einsum('re,erd->rd', mixing, expert_rows, precision=lax.Precision.HIGHEST)
    return (hidden_wide + mixture).astype(jnp.bfloat16)
```

```python
import functools
import math

import jax
import jax.numpy as jnp
from jax import lax
from jax.experimental import pallas as pl
from jax.experimental.pallas import tpu as pltpu
from jax.sharding import PartitionSpec as P

route_scale = 2.5
f32 = jnp.float32
bf16 = jnp.bfloat16
VMEM_LIMIT = 48 * 1024 * 1024


def iota(shape, dim):
    return lax.broadcasted_iota(jnp.int32, shape, dim)


def dot(a, b, dims=((1,), (0,))):
    return lax.dot_general(a, b, (dims, ((), ())), preferred_element_type=f32)


def attend_kernel(scale, n_ctx, n_exp, lengths, base, q_ref, k_ref, routes_ref, out_ref, perm_ref, stat_ref):
    step = pl.program_id(0)
    requests = pl.num_programs(0) - 1
    per = q_ref.shape[2]
    rows = n_ctx * per
    width = out_ref.shape[2]
    per_pair = rows // (n_ctx * n_exp)
    chunk = out_ref.shape[1]

    @pl.when(step == 0)
    def _():
        to, frm = iota((rows, rows), 0), iota((rows, rows), 1)
        group = n_ctx * per_pair
        e, c, rest = to // group, (to % group) // per_pair, to % per_pair
        perm_ref[...] = (frm == c * per + e * per_pair + rest).astype(bf16)
        stat_ref[...] = jnp.zeros_like(stat_ref)

    @pl.when(step < requests)
    def _():
        q = dot(perm_ref[...], q_ref[...].reshape(rows, q_ref.shape[3])).astype(bf16)
        k = k_ref[0]
        scores = dot(q, k, ((1,), (1,))) * scale
        block = k.shape[0]
        row = iota((rows, 1), 0)
        limit = lengths[step] + (row // 2) % 2 - base[0]
        visible = iota((rows, block), 1) < limit
        masked = jnp.where(visible, scores, -1e30)
        top = jnp.max(masked, axis=1, keepdims=True).astype(bf16).astype(f32)
        weights = jnp.where(visible, jnp.exp(masked - top), 0.0)
        total = jnp.sum(weights, axis=1, keepdims=True)
        got = dot(weights.astype(bf16), k[:, :width])
        out_ref[...] = got.astype(bf16).reshape(n_exp, chunk, width)
        here = (iota((chunk, width), 1) == step * chunk + iota((chunk, width), 0))[None]
        stat_ref[0] += jnp.sum(jnp.where(here, top.reshape(n_exp, chunk, 1), 0.0), axis=1)
        stat_ref[1] += jnp.sum(jnp.where(here, total.reshape(n_exp, chunk, 1), 0.0), axis=1)

    @pl.when(step == requests)
    def _():
        top, total = stat_ref[0], stat_ref[1]
        high = total.astype(bf16).astype(f32)
        row = iota((n_exp, chunk, width), 1)
        table = jnp.where(row == 0, top[:, None, :], 0.0)
        table = jnp.where(row == 1, high[:, None, :], table)
        table = jnp.where(row == 2, (total - high)[:, None, :], table)
        table = jnp.where(row == 3, routes_ref[...][None], table)
        out_ref[...] = table.astype(bf16)


def attend(queries, cache, lengths, base, routes_row, scale, n_exp, lat):
    n_ctx, reqs, per, depth = queries.shape
    block = cache.shape[1]
    rows = n_ctx * per
    chunk = rows // n_exp
    last = reqs - 1
    return pl.pallas_call(
        functools.partial(attend_kernel, scale, n_ctx, n_exp),
        out_shape=jax.ShapeDtypeStruct((n_exp, (reqs + 1) * chunk, lat), bf16),
        grid_spec=pltpu.PrefetchScalarGridSpec(
            num_scalar_prefetch=2,
            grid=(reqs + 1,),
            in_specs=[
                pl.BlockSpec((n_ctx, 1, per, depth), lambda r, *_: (0, jnp.minimum(r, last), 0, 0)),
                pl.BlockSpec((1, block, depth), lambda r, *_: (jnp.minimum(r, last), 0, 0)),
                pl.BlockSpec((1, lat), lambda r, *_: (0, 0)),
            ],
            out_specs=pl.BlockSpec((n_exp, chunk, lat), lambda r, *_: (0, r, 0)),
            scratch_shapes=[pltpu.VMEM((rows, rows), bf16), pltpu.VMEM((2, n_exp, lat), f32)],
        ),
        compiler_params=pltpu.CompilerParams(vmem_limit_bytes=VMEM_LIMIT),
        name="attend",
    )(lengths, base, queries, cache, routes_row)


def merge_kernel(n_ctx, in_ref, out_ref, sum_ref):
    sources, _, width = in_ref.shape
    rows = sum_ref.shape[0]
    chunk = in_ref.shape[1] - rows
    reqs = rows // chunk
    part = chunk // n_ctx
    own = reqs * part
    table = in_ref[:, rows : rows + 16, :].astype(f32)
    tops = table[:, 0, :]
    sums = table[:, 1, :] + table[:, 2, :]
    top = jnp.max(tops, axis=0, keepdims=True)
    factor = jnp.exp(tops - top)
    total = jnp.sum(factor * sums, axis=0, keepdims=True)
    columns = factor.T
    for r in range(reqs):
        lo = r * chunk
        acc = jnp.zeros((chunk, width), f32)
        for s in range(sources):
            acc += in_ref[s, lo : lo + chunk, :].astype(f32) * columns[lo : lo + chunk, s : s + 1]
        sum_ref[lo : lo + chunk, :] = acc.astype(bf16)
    to, frm = iota((rows, rows), 0), iota((rows, rows), 1)
    c, r, rest = to // own, (to % own) // part, to % part
    perm = (frm == r * chunk + c * part + rest).astype(bf16)
    out_ref[:, :own, :] = dot(perm, sum_ref[...]).astype(bf16).reshape(n_ctx, own, width)
    high = total.astype(bf16).astype(f32)
    row = iota((16, rows), 0)
    packed = jnp.where(row == 0, top, 0.0)
    packed = jnp.where(row == 1, high, packed)
    packed = jnp.where(row == 2, total - high, packed)
    moved = dot(packed.astype(bf16), perm, ((1,), (1,))).astype(bf16)
    out_ref[:, own : own + 16, :] = jnp.broadcast_to(moved[None], (n_ctx, 16, rows))


def merge(arrived, n_ctx, reqs):
    n_exp, tall, lat = arrived.shape
    chunk = tall // (reqs + 1)
    rows = reqs * chunk
    own = rows // n_ctx
    return pl.pallas_call(
        functools.partial(merge_kernel, n_ctx),
        out_shape=jax.ShapeDtypeStruct((n_ctx, own + 16, lat), bf16),
        scratch_shapes=[pltpu.VMEM((rows, lat), bf16)],
        compiler_params=pltpu.CompilerParams(vmem_limit_bytes=VMEM_LIMIT),
        name="merge",
    )(arrived)


def project_kernel(place, in_ref, up_ref, proj_ref, out_ref, head_ref):
    sources, tall, lat = in_ref.shape
    own = tall - 16
    heads, _, vdim = up_ref.shape

    @pl.when(pl.program_id(0) == 0)
    def _():
        mine = (iota((own, lat), 1) == place[0] * own + iota((own, lat), 0)).astype(bf16)
        table = in_ref[:, own : own + 16, :]
        tops = dot(mine, table[:, 0, :], ((1,), (1,)))
        sums = dot(mine, table[:, 1, :], ((1,), (1,))) + dot(mine, table[:, 2, :], ((1,), (1,)))
        factor = jnp.exp(tops - jnp.max(tops, axis=1, keepdims=True))
        total = jnp.sum(factor * sums, axis=1, keepdims=True)
        acc = jnp.zeros((own, lat), f32)
        for s in range(sources):
            acc += in_ref[s, :own, :].astype(f32) * factor[:, s : s + 1]
        context = (acc / total).astype(bf16)
        for h in range(heads):
            value = dot(context, up_ref[h]).astype(bf16)
            pick = (iota((own // heads, own), 1) == heads * iota((own // heads, own), 0) + h).astype(bf16)
            head_ref[:, h * vdim : (h + 1) * vdim] = dot(pick, value).astype(bf16)

    out_ref[0] = dot(head_ref[...], proj_ref[...]).astype(bf16)


def project(arrived, place, value_up, out_proj, n_ctx):
    sources, tall, lat = arrived.shape
    heads, _, vdim = value_up.shape
    model = out_proj.shape[1]
    cols = model // n_ctx
    rows = (tall - 16) // heads
    return pl.pallas_call(
        project_kernel,
        out_shape=jax.ShapeDtypeStruct((n_ctx, rows, cols), bf16),
        grid_spec=pltpu.PrefetchScalarGridSpec(
            num_scalar_prefetch=1,
            grid=(n_ctx,),
            in_specs=[
                pl.BlockSpec((sources, tall, lat), lambda c, *_: (0, 0, 0)),
                pl.BlockSpec((heads, lat, vdim), lambda c, *_: (0, 0, 0)),
                pl.BlockSpec((heads * vdim, cols), lambda c, *_: (0, c)),
            ],
            out_specs=pl.BlockSpec((1, rows, cols), lambda c, *_: (c, 0, 0)),
            scratch_shapes=[pltpu.VMEM((rows, heads * vdim), bf16)],
        ),
        compiler_params=pltpu.CompilerParams(vmem_limit_bytes=VMEM_LIMIT),
        name="project",
    )(place, arrived, value_up, out_proj)


def expert_kernel(me, hid_ref, gain_ref, router_ref, routes_ref, gate_ref, up_ref, down_ref, out_ref):
    blocks, rows, cols = hid_ref.shape
    experts = router_ref.shape[1]
    square = jnp.zeros((rows, 1), f32)
    for c in range(blocks):
        h = hid_ref[c].astype(f32)
        square += jnp.sum(h * h, axis=1, keepdims=True)
    inverse = lax.rsqrt(square / (blocks * cols) + 1e-06)
    gate = jnp.zeros((rows, gate_ref.shape[2]), f32)
    up = jnp.zeros((rows, up_ref.shape[2]), f32)
    logits = jnp.zeros((rows, experts), f32)
    for c in range(blocks):
        normed = (hid_ref[c].astype(f32) * inverse * gain_ref[c].astype(f32)).astype(bf16)
        gate += dot(normed, gate_ref[c])
        up += dot(normed, up_ref[c])
        logits += dot(normed, router_ref[c], ((1,), (1,)))
    affinity = jax.nn.sigmoid(logits)
    lane = iota((rows, experts), 1)
    mine = jnp.zeros((rows, 1), f32)
    whole = jnp.zeros((rows, 1), f32)
    for k in range(routes_ref.shape[1]):
        choice = routes_ref[:, k : k + 1]
        picked = jnp.sum(jnp.where(lane == choice, affinity, 0.0), axis=1, keepdims=True)
        whole += picked
        mine += jnp.where(choice == me[0], picked, 0.0)
    weight = route_scale * mine / whole
    active = (gate / (1.0 + jnp.exp(-gate)) * up).astype(bf16)
    for c in range(blocks):
        got = dot(active, down_ref[:, c * cols : (c + 1) * cols])
        out_ref[c] = (got * weight).astype(bf16)


def experts_here(hidden, gain, router, routes, me, gate, up, down):
    vmem = pl.BlockSpec(memory_space=pltpu.VMEM)
    return pl.pallas_call(
        expert_kernel,
        out_shape=jax.ShapeDtypeStruct(hidden.shape, bf16),
        in_specs=[pl.BlockSpec(memory_space=pltpu.SMEM)] + [vmem] * 7,
        out_specs=vmem,
        compiler_params=pltpu.CompilerParams(vmem_limit_bytes=VMEM_LIMIT),
        name="experts",
    )(me, hidden, gain, router, routes, gate, up, down)


def on_device(
    queries,
    latent_cache,
    context_lengths,
    value_up,
    out_proj,
    residual,
    norm_gain,
    router,
    routes,
    expert_gate,
    expert_up,
    expert_down,
):
    reqs, pair, heads, depth = queries.shape
    lat, vdim = value_up.shape[1:]
    scale = 1.0 / math.sqrt(vdim + depth - lat)
    n_ctx, n_exp = lax.axis_size("ctx"), lax.axis_size("exp")
    n_all = n_ctx * n_exp
    everyone = ("ctx", "exp")
    ctx, exp = lax.axis_index("ctx"), lax.axis_index("exp")
    own_rows, model = residual.shape
    top = routes.shape[1]
    cols = model // n_ctx
    experts = router.shape[1]

    def swap(x, axes):
        return lax.all_to_all(x, axes, split_axis=0, concat_axis=0, tiled=True)

    q = queries.reshape(reqs * pair * heads, depth)
    q = swap(jnp.broadcast_to(q[None], (n_exp, *q.shape)), "exp")
    q = q.reshape(n_exp, reqs, pair * heads, depth).transpose(1, 0, 2, 3)
    q = lax.all_gather(q.reshape(reqs, n_exp * pair * heads, depth), "ctx", axis=0)

    base = ((ctx * n_exp + exp) * latent_cache.shape[1]).reshape(1)
    routes_row = jnp.zeros((1, lat), f32).at[0, : own_rows * top].set(routes.reshape(-1).astype(f32))
    sent = attend(q, latent_cache, context_lengths, base, routes_row, scale, n_exp, lat)
    arrived = swap(sent, "exp")
    table_row = arrived.shape[1] // (reqs + 1) * reqs + 3
    all_routes = arrived[:, table_row, : own_rows * top].astype(jnp.int32).reshape(n_exp * own_rows, top)
    arrived = swap(merge(arrived, n_ctx, reqs), "ctx")
    terms = project(arrived, ctx.reshape(1), value_up, out_proj, n_ctx)

    terms = swap(terms.reshape(n_all, own_rows, cols), everyone)
    attention = jnp.sum(terms.astype(f32), axis=0)
    own = lax.dynamic_slice_in_dim(residual, ctx * cols, cols, 1)
    hidden = (own.astype(f32) + attention).astype(bf16)
    rows = swap(jnp.broadcast_to(hidden[None], (n_all, own_rows, cols)), everyone)
    mixed = experts_here(
        rows.reshape(n_ctx, n_exp * own_rows, cols),
        norm_gain.reshape(n_ctx, 1, cols),
        router.T.reshape(experts, n_ctx, cols).transpose(1, 0, 2),
        all_routes,
        exp.reshape(1),
        expert_gate.reshape(n_ctx, cols, -1),
        expert_up.reshape(n_ctx, cols, -1),
        expert_down[0],
    )
    mixed = swap(mixed.reshape(n_all, own_rows, cols), everyone)
    mixture = jnp.sum(mixed.astype(f32), axis=0)
    return (hidden.astype(f32) + mixture).astype(bf16)


def solution(mesh):
    return jax.shard_map(
        on_device,
        mesh=mesh,
        in_specs=(
            P("req", None, ("ctx", "exp"), None),
            P("req", ("ctx", "exp"), None),
            P("req"),
            P(("ctx", "exp"), None, None),
            P(("ctx", "exp"), None),
            P(("req", "exp"), None),
            P(),
            P(),
            P(("req", "exp"), None),
            P("exp", None, "ctx"),
            P("exp", None, "ctx"),
            P("exp", "ctx", None),
        ),
        out_specs=P(("req", "exp"), "ctx"),
        check_vma=False,
    )
```

```python
import functools
import math

import jax
import jax.numpy as jnp
from jax import lax
from jax.experimental import pallas as pl
from jax.experimental.pallas import tpu as pltpu
from jax.sharding import PartitionSpec as P

route_scale = 2.5
f32 = jnp.float32
bf16 = jnp.bfloat16
VMEM_LIMIT = 16 * 1024 * 1024
LANES = 128
LOG2E = math.log2(math.e)
TABLE = 16


def iota(shape, dim):
    return lax.broadcasted_iota(jnp.int32, shape, dim)


def dot(a, b, dims=((1,), (0,))):
    return lax.dot_general(a, b, (dims, ((), ())), preferred_element_type=f32)


def in_hbm(x):
    return pltpu.with_memory_space_constraint(x, pltpu.HBM)


def attend_kernel(scale, n_ctx, n_exp, first, permuted, lengths, base, q_ref, k_ref, routes_ref, out_ref, *scratch):
    stat_ref, buf_ref, table_ref, sems = scratch[:4]
    step = pl.program_id(0)
    slot = lax.rem(step, 2)
    n_outer, unroll, per, depth = q_ref.shape
    rows = n_outer * per
    chunk = rows // n_exp
    block = k_ref.shape[2]
    tall = out_ref.shape[1] - TABLE
    lines = stat_ref.shape[2] // LANES
    tiles = tall // (unroll * pl.num_programs(0) * chunk)
    width = tiles * LANES

    @pl.when(step == 0)
    def _():
        stat_ref[...] = jnp.zeros_like(stat_ref)
        if permuted:
            per_pair = rows // (n_ctx * n_exp)
            to, frm = iota((rows, rows), 0), iota((rows, rows), 1)
            e, c, rest = to // chunk, (to % chunk) // per_pair, to % per_pair
            scratch[4][...] = (frm == c * per + e * per_pair + rest).astype(bf16)

    row = iota((rows, 1), 0)
    lane = iota((rows, block), 1)
    span = buf_ref.shape[2]

    def leave(which, where):
        place = out_ref.at[:, pl.ds(pl.multiple_of(where * span, span), span), :]
        return pltpu.make_async_copy(buf_ref.at[which], place, sems.at[which])

    @pl.when(step >= 2)
    def _():
        leave(slot, step - 2).wait()

    for u in range(unroll):
        r = step * unroll + u
        q = q_ref[:, u].reshape(rows, depth)
        if permuted:
            q = dot(scratch[4][...], q).astype(bf16)
        k = k_ref[u]
        scores = dot(q, k) * (scale * LOG2E)
        visible = lane < lengths[first + r] + (row // 2) % 2 - base[0]
        masked = jnp.where(visible, scores, -1e30)
        top = jnp.maximum(jnp.max(masked, axis=1, keepdims=True), -1e29).astype(bf16).astype(f32)
        weights = jnp.exp2(masked - top)
        total = jnp.sum(weights, axis=1, keepdims=True)
        got = dot(weights.astype(bf16), k[:width], ((1,), (1,)))
        got = got.astype(bf16).reshape(n_exp, chunk, width)
        for t in range(tiles):
            lo = (u * tiles + t) * chunk
            buf_ref[slot, :, lo : lo + chunk, :] = got[:, :, t * LANES : (t + 1) * LANES]
        spot = iota((chunk, lines * LANES), 1) == r * chunk + iota((chunk, lines * LANES), 0)
        spot = spot[None]
        stat_ref[0] += jnp.sum(jnp.where(spot, top.reshape(n_exp, chunk, 1), 0.0), axis=1)
        stat_ref[1] += jnp.sum(jnp.where(spot, total.reshape(n_exp, chunk, 1), 0.0), axis=1)

    leave(slot, step).start()

    @pl.when(step == pl.num_programs(0) - 1)
    def _():
        top, total = stat_ref[0], stat_ref[1]
        high = total.astype(bf16).astype(f32)
        line = iota((n_exp, TABLE, LANES), 1)
        table = jnp.where(line == TABLE - 1, routes_ref[...][None], 0.0)
        for kind, values in enumerate((top, high, total - high)):
            for w in range(lines):
                part = values[:, w * LANES : (w + 1) * LANES]
                table = jnp.where(line == kind * lines + w, part[:, None, :], table)
        table_ref[...] = table.astype(bf16)
        last = pltpu.make_async_copy(table_ref, out_ref.at[:, pl.ds(tall, TABLE), :], sems.at[2])
        last.start()

        @pl.when(step >= 1)
        def _():
            leave(1 - slot, step - 1).wait()

        leave(slot, step).wait()
        last.wait()


def attend(queries, cache, lengths, base, routes_row, scale, n_ctx, n_exp, lat, first, permuted):
    n_outer, reqs, per, depth = queries.shape
    block = cache.shape[2]
    rows = n_outer * per
    unroll = 2 if reqs % 2 == 0 and first % 2 == 0 else 1
    chunk = rows // n_exp
    tall = reqs * chunk * (lat // LANES) + TABLE
    wide = -(-reqs * chunk // LANES) * LANES
    return pl.pallas_call(
        functools.partial(attend_kernel, scale, n_ctx, n_exp, first, permuted),
        out_shape=pltpu.HBM((n_exp, tall, LANES), bf16),
        grid_spec=pltpu.PrefetchScalarGridSpec(
            num_scalar_prefetch=2,
            grid=(reqs // unroll,),
            in_specs=[
                pl.BlockSpec((n_outer, unroll, per, depth), lambda r, *_: (0, r, 0, 0)),
                pl.BlockSpec((unroll, depth, block), lambda r, *_: (r + first // unroll, 0, 0)),
                pl.BlockSpec((1, LANES), lambda r, *_: (0, 0)),
            ],
            out_specs=pl.BlockSpec(memory_space=pltpu.HBM),
            scratch_shapes=[
                pltpu.VMEM((2, n_exp, wide), f32),
                pltpu.VMEM((2, n_exp, unroll * chunk * (lat // LANES), LANES), bf16),
                pltpu.VMEM((n_exp, TABLE, LANES), bf16),
                pltpu.SemaphoreType.DMA((3,)),
            ]
            + ([pltpu.VMEM((rows, rows), bf16)] if permuted else []),
        ),
        compiler_params=pltpu.CompilerParams(vmem_limit_bytes=VMEM_LIMIT),
        cost_estimate=pl.CostEstimate(
            flops=4 * reqs * rows * block * depth,
            bytes_accessed=2 * reqs * (depth * block + rows * (depth + lat)),
            transcendentals=reqs * rows * block,
        ),
        name="attend",
    )(lengths, base, queries, cache, routes_row)


def merge_rows(in_ref, sum_ref, first, count):
    sources, tall, _ = in_ref.shape
    tall -= TABLE
    tiles = sum_ref.shape[1] // LANES
    chunk = tall // (count * tiles)
    lines = -(-count * chunk // LANES)
    table = in_ref[:, tall : tall + TABLE, :].astype(f32)

    def kind(n):
        return jnp.concatenate([table[:, n * lines + w, :] for w in range(lines)], axis=1)

    tops, sums = kind(0), kind(1) + kind(2)
    top = jnp.max(tops, axis=0, keepdims=True)
    factor = jnp.exp2(tops - top)
    columns = factor.T
    for r in range(count):
        lo = r * chunk
        for t in range(tiles):
            acc = jnp.zeros((chunk, LANES), f32)
            for s in range(sources):
                at = (r * tiles + t) * chunk
                acc += in_ref[s, at : at + chunk, :].astype(f32) * columns[lo : lo + chunk, s : s + 1]
            sum_ref[first + lo : first + lo + chunk, t * LANES : (t + 1) * LANES] = acc.astype(bf16)
    total = jnp.sum(factor * sums, axis=0, keepdims=True)
    return top[:, : count * chunk], total[:, : count * chunk], table[:, TABLE - 1, :]


def merge_early_kernel(count, in_ref, sum_ref, stat_ref, routes_ref):
    top, total, routes_ref[...] = merge_rows(in_ref, sum_ref, 0, count)
    line = iota(stat_ref.shape, 0)
    stat_ref[...] = jnp.where(line == 0, top, jnp.where(line == 1, total, 0.0))


def merge_early(arrived, count, lat):
    sources, tall, _ = arrived.shape
    rows = (tall - TABLE) // (lat // LANES)
    return pl.pallas_call(
        functools.partial(merge_early_kernel, count),
        out_shape=(
            jax.ShapeDtypeStruct((rows, lat), bf16),
            jax.ShapeDtypeStruct((8, rows), f32),
            jax.ShapeDtypeStruct((sources, LANES), f32),
        ),
        compiler_params=pltpu.CompilerParams(vmem_limit_bytes=VMEM_LIMIT),
        cost_estimate=pl.CostEstimate(
            flops=4 * arrived.size, bytes_accessed=2 * arrived.size, transcendentals=sources * rows
        ),
        name="merge_early",
    )(arrived)


def merge_late_kernel(n_ctx, count, early_ref, stat_ref, in_ref, far_ref, out_ref, sum_ref, up_ref, sem):
    rows, lat = sum_ref.shape
    first = early_ref.shape[0]
    fetch = pltpu.make_async_copy(far_ref, up_ref, sem)
    fetch.start()
    heads = up_ref.shape[1]
    reqs = count * rows // (rows - first)
    sum_ref[:first, :] = early_ref[...]
    top, total, _ = merge_rows(in_ref, sum_ref, first, count)
    top = jnp.concatenate([stat_ref[0:1, :], top], axis=1)
    total = jnp.concatenate([stat_ref[1:2, :], total], axis=1)
    own = rows // n_ctx
    part = own // reqs
    pairs = own // heads
    pair = part // heads
    to, frm = iota((rows, rows), 0), iota((rows, rows), 1)
    c, h, r, j = to // own, (to % own) // pairs, (to % pairs) // pair, to % pair
    perm = (frm == r * n_ctx * part + c * part + j * heads + h).astype(bf16)
    moved = dot(perm, sum_ref[...]).astype(bf16)
    fetch.wait()
    for c in range(n_ctx):
        for h in range(heads):
            lo = c * own + h * pairs
            value = dot(moved[lo : lo + pairs], up_ref[c, h])
            out_ref[c, h * pairs : (h + 1) * pairs, :] = value.astype(bf16)
    high = total.astype(bf16).astype(f32)
    line = iota((TABLE, rows), 0)
    packed = jnp.where(line == 0, top, 0.0)
    packed = jnp.where(line == 1, high, packed)
    packed = jnp.where(line == 2, total - high, packed)
    table = dot(packed.astype(bf16), perm, ((1,), (1,))).astype(bf16)
    for c in range(n_ctx):
        lo = c * own // LANES * LANES
        out_ref[c, own : own + TABLE, :] = table[:, lo : lo + LANES]


def merge_late(early, stats, arrived, value_up, count):
    n_ctx, heads, lat, vdim = value_up.shape
    rows = early.shape[0] + (arrived.shape[1] - TABLE) // (lat // LANES)
    return pl.pallas_call(
        functools.partial(merge_late_kernel, n_ctx, count),
        out_shape=jax.ShapeDtypeStruct((n_ctx, rows // n_ctx + TABLE, vdim), bf16),
        in_specs=[pl.BlockSpec(memory_space=pltpu.VMEM)] * 3 + [pl.BlockSpec(memory_space=pltpu.HBM)],
        scratch_shapes=[
            pltpu.VMEM((rows, lat), bf16),
            pltpu.VMEM((n_ctx, heads, lat, vdim), bf16),
            pltpu.SemaphoreType.DMA,
        ],
        compiler_params=pltpu.CompilerParams(vmem_limit_bytes=VMEM_LIMIT),
        name="merge_late",
    )(early, stats, arrived, in_hbm(value_up))


def project_kernel(place, in_ref, far_ref, out_ref, proj_ref, sum_ref, sems):
    sources, tall, vdim = in_ref.shape
    own = tall - TABLE
    blocks, rows, cols = out_ref.shape
    heads = own // rows
    copies = []
    for h in range(heads):
        part = pl.ds(h * vdim, vdim)
        copies.append(pltpu.make_async_copy(far_ref.at[part], proj_ref.at[part], sems.at[h]))
        copies[h].start()
    offset = lax.rem(place[0] * own, LANES)
    mine = (iota((own, LANES), 1) == offset + iota((own, LANES), 0)).astype(bf16)
    table = in_ref[:, own : own + TABLE, :]
    tops = dot(mine, table[:, 0, :], ((1,), (1,)))
    sums = dot(mine, table[:, 1, :], ((1,), (1,))) + dot(mine, table[:, 2, :], ((1,), (1,)))
    factor = jnp.exp2(tops - jnp.max(tops, axis=1, keepdims=True))
    total = jnp.sum(factor * sums, axis=1, keepdims=True)
    acc = jnp.zeros((own, vdim), f32)
    for s in range(sources):
        acc += in_ref[s, :own, :].astype(f32) * factor[:, s : s + 1]
    value = (acc / total).astype(bf16)
    for h in range(heads):
        copies[h].wait()
        for c in range(blocks):
            weight = proj_ref[h * vdim : (h + 1) * vdim, c * cols : (c + 1) * cols]
            term = dot(value[h * rows : (h + 1) * rows], weight)
            if h > 0:
                term += sum_ref[c]
            if h < heads - 1:
                sum_ref[c] = term
            else:
                out_ref[c] = term.astype(bf16)


def project(arrived, place, out_proj, n_ctx):
    sources, tall, vdim = arrived.shape
    depth, model = out_proj.shape
    cols = model // n_ctx
    rows = (tall - TABLE) * vdim // depth
    vmem = pl.BlockSpec(memory_space=pltpu.VMEM)
    return pl.pallas_call(
        project_kernel,
        out_shape=jax.ShapeDtypeStruct((n_ctx, rows, cols), bf16),
        in_specs=[pl.BlockSpec(memory_space=pltpu.SMEM), vmem, pl.BlockSpec(memory_space=pltpu.HBM)],
        out_specs=vmem,
        scratch_shapes=[
            pltpu.VMEM(out_proj.shape, bf16),
            pltpu.VMEM((n_ctx, rows, cols), f32),
            pltpu.SemaphoreType.DMA((depth // vdim,)),
        ],
        compiler_params=pltpu.CompilerParams(vmem_limit_bytes=VMEM_LIMIT),
        name="project",
    )(place, arrived, in_hbm(out_proj))


def expert_kernel(me, hid_ref, gain_ref, router_ref, routes_ref, gate_ref, *refs):
    far_refs, out_ref, (up_ref, down_ref, normed_ref, sems) = refs[:2], refs[2], refs[3:]
    blocks, rows, cols = hid_ref.shape
    experts = router_ref.shape[1]
    half_up, half_down = blocks // 2, down_ref.shape[0] // 2
    pieces = [(0, pl.ds(0, half_up)), (0, pl.ds(half_up, blocks - half_up))]
    pieces += [(1, pl.ds(0, half_down)), (1, pl.ds(half_down, half_down))]
    copies = [
        pltpu.make_async_copy(far_refs[n].at[piece], (up_ref, down_ref)[n].at[piece], sems.at[i])
        for i, (n, piece) in enumerate(pieces)
    ]
    for copy in copies:
        copy.start()
    square = jnp.zeros((rows, 1), f32)
    for c in range(blocks):
        h = hid_ref[c].astype(f32)
        square += jnp.sum(h * h, axis=1, keepdims=True)
    inverse = lax.rsqrt(square / (blocks * cols) + 1e-06)
    gate = jnp.zeros((rows, gate_ref.shape[2]), f32)
    up = jnp.zeros((rows, up_ref.shape[2]), f32)
    logits = jnp.zeros((rows, experts), f32)
    for c in range(blocks):
        normed = (hid_ref[c].astype(f32) * inverse * gain_ref[c].astype(f32)).astype(bf16)
        gate += dot(normed, gate_ref[c])
        logits += dot(normed, router_ref[c], ((1,), (1,)))
        normed_ref[c] = normed
    for c in range(blocks):
        if c == 0 or c == half_up:
            copies[c // half_up].wait()
        up += dot(normed_ref[c], up_ref[c])
    affinity = jax.nn.sigmoid(logits)
    lane = iota((rows, experts), 1)
    mine = jnp.zeros((rows, 1), f32)
    whole = jnp.zeros((rows, 1), f32)
    for k in range(routes_ref.shape[1]):
        choice = routes_ref[:, k : k + 1]
        picked = jnp.sum(jnp.where(lane == choice, affinity, 0.0), axis=1, keepdims=True)
        whole += picked
        mine += jnp.where(choice == me[0], picked, 0.0)
    weight = route_scale * mine / whole
    copies[2].wait()
    copies[3].wait()
    active = (gate / (1.0 + jnp.exp(-gate)) * up).astype(bf16)
    for c in range(blocks):
        got = dot(active, down_ref[:, c * cols : (c + 1) * cols])
        out_ref[c] = (got * weight).astype(bf16)


def experts_here(hidden, gain, router, routes, me, gate, up, down):
    vmem = pl.BlockSpec(memory_space=pltpu.VMEM)
    return pl.pallas_call(
        expert_kernel,
        out_shape=jax.ShapeDtypeStruct(hidden.shape, bf16),
        in_specs=[pl.BlockSpec(memory_space=pltpu.SMEM)]
        + [vmem] * 5
        + [pl.BlockSpec(memory_space=pltpu.HBM)] * 2,
        out_specs=vmem,
        scratch_shapes=[
            pltpu.VMEM(up.shape, bf16),
            pltpu.VMEM(down.shape, bf16),
            pltpu.VMEM(hidden.shape, bf16),
            pltpu.SemaphoreType.DMA((4,)),
        ],
        compiler_params=pltpu.CompilerParams(vmem_limit_bytes=VMEM_LIMIT),
        name="experts",
    )(me, hidden, gain, router, routes, gate, in_hbm(up), in_hbm(down))


def on_device(
    queries,
    latent_cache,
    context_lengths,
    value_up,
    out_proj,
    residual,
    norm_gain,
    router,
    routes,
    expert_gate,
    expert_up,
    expert_down,
):
    reqs, pair, heads, depth = queries.shape
    lat, vdim = value_up.shape[1:]
    scale = 1.0 / math.sqrt(vdim + depth - lat)
    n_ctx, n_exp = lax.axis_size("ctx"), lax.axis_size("exp")
    n_all = n_ctx * n_exp
    everyone = ("ctx", "exp")
    ctx, exp = lax.axis_index("ctx"), lax.axis_index("exp")
    own_rows, model = residual.shape
    top = routes.shape[1]
    cols = model // n_ctx
    experts = router.shape[1]

    def swap(x, axes):
        return lax.all_to_all(x, axes, split_axis=0, concat_axis=0, tiled=True)

    def spread(x, axes, size):
        return swap(jnp.broadcast_to(x[None], (size, *x.shape)), axes)

    early = reqs * 5 // 16
    counts = (early, reqs - early)
    per = pair * heads
    q = queries.reshape(reqs * per, depth)
    late = spread(q[early * per :], "exp", n_exp)
    late = late.reshape(n_exp, counts[1], per, depth).transpose(1, 0, 2, 3).reshape(counts[1], n_exp * per, depth)
    q, late = lax.optimization_barrier((q[: early * per], late))
    late = lax.all_gather(late, "ctx", axis=0)
    q = spread(q, "ctx", n_ctx)
    q = q.reshape(n_ctx, early, per, depth).transpose(1, 0, 2, 3).reshape(early * n_ctx * per, depth)
    q = spread(q, "exp", n_exp).reshape(n_exp, early, n_ctx * per, depth)

    base = ((ctx * n_exp + exp) * latent_cache.shape[1]).reshape(1)
    routes_row = jnp.zeros((1, LANES), f32).at[0, : own_rows * top].set(routes.reshape(-1).astype(f32))
    cache = in_hbm(latent_cache.swapaxes(1, 2))
    rest = (cache, context_lengths, base, routes_row, scale, n_ctx, n_exp, lat)
    sent = attend(q, *rest, 0, False)
    up, late = lax.optimization_barrier((value_up, late))
    all_up = lax.all_gather(up, "ctx", axis=0)
    late = in_hbm(late)
    arrived = swap(sent, "exp")
    sent, arrived = lax.optimization_barrier((attend(late, *rest, early, True), arrived))
    sums, stats, route_rows = merge_early(arrived, early, lat)
    all_routes = route_rows[:, : own_rows * top].astype(jnp.int32).reshape(n_exp, own_rows, top)
    sent, sums = lax.optimization_barrier((sent, sums))
    arrived = swap(sent, "exp")
    arrived = swap(merge_late(sums, stats, arrived, all_up, reqs - early), "ctx")
    terms = project(arrived, ctx.reshape(1), out_proj, n_ctx)

    terms = swap(terms.reshape(n_all, own_rows, cols), everyone)
    attention = jnp.sum(terms.astype(f32), axis=0)
    own = lax.dynamic_slice_in_dim(residual, ctx * cols, cols, 1)
    hidden = (own.astype(f32) + attention).astype(bf16)

    slots = max(2, own_rows * top // experts)
    before = jnp.tril(jnp.ones((own_rows, own_rows), jnp.int32), -1)

    def slot_of(named, axis):
        shape = (1,) * axis + (own_rows, own_rows) + (1,) * (named.ndim - 1 - axis)
        earlier = jnp.sum(before.reshape(shape) * jnp.expand_dims(named, axis), axis=axis + 1)
        return jnp.where(named == 1, earlier, -1)

    named = jnp.sum((routes[:, :, None] == jnp.arange(experts)).astype(jnp.int32), axis=1)
    place = (slot_of(named, 0)[:, :, None] == jnp.arange(slots)).astype(bf16)
    place = jnp.broadcast_to(place[:, None], (own_rows, n_ctx, experts, slots)).reshape(own_rows, -1)
    rows = dot(place, hidden, ((0,), (0,))).astype(bf16)
    rows = swap(rows.reshape(n_all, slots, cols), everyone)

    named = jnp.any(all_routes == exp, axis=2).astype(jnp.int32)
    taken = (slot_of(named, 1)[:, None, :] == jnp.arange(slots)[None, :, None]).astype(jnp.int32)
    slot_routes = jnp.sum(taken[..., None] * all_routes[:, None], axis=2).reshape(n_exp * slots, top)
    mixed = experts_here(
        rows.reshape(n_ctx, n_exp * slots, cols),
        norm_gain.reshape(n_ctx, 1, cols),
        router.T.reshape(experts, n_ctx, cols).transpose(1, 0, 2),
        slot_routes,
        exp.reshape(1),
        expert_gate.reshape(n_ctx, cols, -1),
        expert_up.reshape(n_ctx, cols, -1),
        expert_down[0],
    )
    mixed = swap(mixed.reshape(n_all, slots, cols), everyone)
    mixture = dot(place, mixed.reshape(n_all * slots, cols))
    return (hidden.astype(f32) + mixture).astype(bf16)


def solution(mesh):
    return jax.shard_map(
        on_device,
        mesh=mesh,
        in_specs=(
            P("req", None, ("ctx", "exp"), None),
            P("req", ("ctx", "exp"), None),
            P("req"),
            P(("ctx", "exp"), None, None),
            P(("ctx", "exp"), None),
            P(("req", "exp"), None),
            P(),
            P(),
            P(("req", "exp"), None),
            P("exp", None, "ctx"),
            P("exp", None, "ctx"),
            P("exp", "ctx", None),
        ),
        out_specs=P(("req", "exp"), "ctx"),
        check_vma=False,
    )
```

```python
import functools
import math

import jax
import jax.numpy as jnp
from jax import lax
from jax.experimental import pallas as pl
from jax.experimental.pallas import tpu as pltpu
from jax.sharding import PartitionSpec as P

route_scale = 2.5
f32 = jnp.float32
bf16 = jnp.bfloat16
VMEM_LIMIT = 16 * 1024 * 1024
LANES = 128
AHEAD = 4
LOG2E = math.log2(math.e)
TABLE = 16


def iota(shape, dim):
    return lax.broadcasted_iota(jnp.int32, shape, dim)


def dot(a, b, dims=((1,), (0,))):
    return lax.dot_general(a, b, (dims, ((), ())), preferred_element_type=f32)


def in_hbm(x):
    return pltpu.with_memory_space_constraint(x, pltpu.HBM)


def attend_kernel(scale, n_ctx, n_exp, first, permuted, steps, lengths, base, q_far, k_far, routes_ref, out_ref, *scratch):
    stat_ref, buf_ref, table_ref, sems, q_ref, k_ref, in_sems = scratch[:7]
    step = pl.program_id(0)
    slot = lax.rem(step, 2)
    ahead, n_outer, unroll, per, depth = q_ref.shape
    rows = n_outer * per
    chunk = rows // n_exp
    block = k_ref.shape[3]
    tall = out_ref.shape[1] - TABLE
    lines = stat_ref.shape[2] // LANES
    tiles = tall // (unroll * steps * chunk)
    width = tiles * LANES

    @pl.when(step == 0)
    def _():
        stat_ref[...] = jnp.zeros_like(stat_ref)
        if permuted:
            per_pair = rows // (n_ctx * n_exp)
            to, frm = iota((rows, rows), 0), iota((rows, rows), 1)
            e, c, rest = to // chunk, (to % chunk) // per_pair, to % per_pair
            scratch[7][...] = (frm == c * per + e * per_pair + rest).astype(bf16)

    def bring(where):
        into = lax.rem(where, ahead)
        mine, yours = pl.ds(where * unroll, unroll), pl.ds(first + where * unroll, unroll)
        return (
            pltpu.make_async_copy(q_far.at[:, mine], q_ref.at[into], in_sems.at[0, into]),
            pltpu.make_async_copy(k_far.at[yours], k_ref.at[into], in_sems.at[1, into]),
        )

    @pl.when(step == 0)
    def _():
        for where in range(min(ahead - 1, steps)):
            for copy in bring(where):
                copy.start()

    @pl.when(step + ahead - 1 < steps)
    def _():
        for copy in bring(step + ahead - 1):
            copy.start()

    for copy in bring(step):
        copy.wait()
    now = lax.rem(step, ahead)
    row = iota((rows, 1), 0)
    lane = iota((rows, block), 1)
    span = buf_ref.shape[2]

    def leave(which, where):
        place = out_ref.at[:, pl.ds(pl.multiple_of(where * span, span), span), :]
        return pltpu.make_async_copy(buf_ref.at[which], place, sems.at[which])

    @pl.when(step >= 2)
    def _():
        leave(slot, step - 2).wait()

    for u in range(unroll):
        r = step * unroll + u
        q = q_ref[now, :, u].reshape(rows, depth)
        if permuted:
            q = dot(scratch[7][...], q).astype(bf16)
        k = k_ref[now, u]
        scores = dot(q, k) * (scale * LOG2E)
        visible = lane < lengths[first + r] + (row // 2) % 2 - base[0]
        masked = jnp.where(visible, scores, -1e30)
        top = jnp.maximum(jnp.max(masked, axis=1, keepdims=True), -1e29).astype(bf16).astype(f32)
        weights = jnp.exp2(masked - top)
        total = jnp.sum(weights, axis=1, keepdims=True)
        got = dot(weights.astype(bf16), k[:width], ((1,), (1,)))
        got = got.astype(bf16).reshape(n_exp, chunk, width)
        for t in range(tiles):
            lo = (u * tiles + t) * chunk
            buf_ref[slot, :, lo : lo + chunk, :] = got[:, :, t * LANES : (t + 1) * LANES]
        spot = iota((chunk, lines * LANES), 1) == r * chunk + iota((chunk, lines * LANES), 0)
        spot = spot[None]
        stat_ref[0] += jnp.sum(jnp.where(spot, top.reshape(n_exp, chunk, 1), 0.0), axis=1)
        stat_ref[1] += jnp.sum(jnp.where(spot, total.reshape(n_exp, chunk, 1), 0.0), axis=1)

    leave(slot, step).start()

    @pl.when(step == steps - 1)
    def _():
        top, total = stat_ref[0], stat_ref[1]
        high = total.astype(bf16).astype(f32)
        line = iota((n_exp, TABLE, LANES), 1)
        table = jnp.where(line == TABLE - 1, routes_ref[...][None], 0.0)
        for kind, values in enumerate((top, high, total - high)):
            for w in range(lines):
                part = values[:, w * LANES : (w + 1) * LANES]
                table = jnp.where(line == kind * lines + w, part[:, None, :], table)
        table_ref[...] = table.astype(bf16)
        last = pltpu.make_async_copy(table_ref, out_ref.at[:, pl.ds(tall, TABLE), :], sems.at[2])
        last.start()

        @pl.when(step >= 1)
        def _():
            leave(1 - slot, step - 1).wait()

        leave(slot, step).wait()
        last.wait()


def attend(queries, cache, lengths, base, routes_row, scale, n_ctx, n_exp, lat, first, permuted):
    n_outer, reqs, per, depth = queries.shape
    block = cache.shape[2]
    rows = n_outer * per
    unroll = 2 if reqs % 2 == 0 and first % 2 == 0 else 1
    chunk = rows // n_exp
    tall = reqs * chunk * (lat // LANES) + TABLE
    wide = -(-reqs * chunk // LANES) * LANES
    return pl.pallas_call(
        functools.partial(attend_kernel, scale, n_ctx, n_exp, first, permuted, reqs // unroll),
        out_shape=pltpu.HBM((n_exp, tall, LANES), bf16),
        grid_spec=pltpu.PrefetchScalarGridSpec(
            num_scalar_prefetch=2,
            grid=(reqs // unroll,),
            in_specs=[
                pl.BlockSpec(memory_space=pl.ANY),
                pl.BlockSpec(memory_space=pl.ANY),
                pl.BlockSpec((1, LANES), lambda r, *_: (0, 0)),
            ],
            out_specs=pl.BlockSpec(memory_space=pltpu.HBM),
            scratch_shapes=[
                pltpu.VMEM((2, n_exp, wide), f32),
                pltpu.VMEM((2, n_exp, unroll * chunk * (lat // LANES), LANES), bf16),
                pltpu.VMEM((n_exp, TABLE, LANES), bf16),
                pltpu.SemaphoreType.DMA((3,)),
                pltpu.VMEM((AHEAD, n_outer, unroll, per, depth), bf16),
                pltpu.VMEM((AHEAD, unroll, depth, block), bf16),
                pltpu.SemaphoreType.DMA((2, AHEAD)),
            ]
            + ([pltpu.VMEM((rows, rows), bf16)] if permuted else []),
        ),
        compiler_params=pltpu.CompilerParams(vmem_limit_bytes=VMEM_LIMIT),
        cost_estimate=pl.CostEstimate(
            flops=4 * reqs * rows * block * depth,
            bytes_accessed=2 * reqs * (depth * block + rows * (depth + lat)),
            transcendentals=reqs * rows * block,
        ),
        name="attend",
    )(lengths, base, queries, cache, routes_row)


def merge_rows(in_ref, sum_ref, first, count):
    sources, tall, _ = in_ref.shape
    tall -= TABLE
    tiles = sum_ref.shape[1] // LANES
    chunk = tall // (count * tiles)
    lines = -(-count * chunk // LANES)
    table = in_ref[:, tall : tall + TABLE, :].astype(f32)

    def kind(n):
        return jnp.concatenate([table[:, n * lines + w, :] for w in range(lines)], axis=1)

    tops, sums = kind(0), kind(1) + kind(2)
    top = jnp.max(tops, axis=0, keepdims=True)
    factor = jnp.exp2(tops - top)
    columns = factor.T
    for r in range(count):
        lo = r * chunk
        for t in range(tiles):
            acc = jnp.zeros((chunk, LANES), f32)
            for s in range(sources):
                at = (r * tiles + t) * chunk
                acc += in_ref[s, at : at + chunk, :].astype(f32) * columns[lo : lo + chunk, s : s + 1]
            sum_ref[first + lo : first + lo + chunk, t * LANES : (t + 1) * LANES] = acc.astype(bf16)
    total = jnp.sum(factor * sums, axis=0, keepdims=True)
    return top[:, : count * chunk], total[:, : count * chunk], table[:, TABLE - 1, :]


def merge_early_kernel(count, in_ref, sum_ref, stat_ref, routes_ref):
    top, total, routes_ref[...] = merge_rows(in_ref, sum_ref, 0, count)
    line = iota(stat_ref.shape, 0)
    stat_ref[...] = jnp.where(line == 0, top, jnp.where(line == 1, total, 0.0))


def merge_early(arrived, count, lat):
    sources, tall, _ = arrived.shape
    rows = (tall - TABLE) // (lat // LANES)
    return pl.pallas_call(
        functools.partial(merge_early_kernel, count),
        out_shape=(
            jax.ShapeDtypeStruct((rows, lat), bf16),
            jax.ShapeDtypeStruct((8, rows), f32),
            jax.ShapeDtypeStruct((sources, LANES), f32),
        ),
        compiler_params=pltpu.CompilerParams(vmem_limit_bytes=VMEM_LIMIT),
        cost_estimate=pl.CostEstimate(
            flops=4 * arrived.size, bytes_accessed=2 * arrived.size, transcendentals=sources * rows
        ),
        name="merge_early",
    )(arrived)


def merge_late_kernel(n_ctx, count, early_ref, stat_ref, in_ref, far_ref, out_ref, sum_ref, up_ref, sem):
    rows, lat = sum_ref.shape
    first = early_ref.shape[0]
    fetch = pltpu.make_async_copy(far_ref, up_ref, sem)
    fetch.start()
    heads = up_ref.shape[1]
    reqs = count * rows // (rows - first)
    sum_ref[:first, :] = early_ref[...]
    top, total, _ = merge_rows(in_ref, sum_ref, first, count)
    top = jnp.concatenate([stat_ref[0:1, :], top], axis=1)
    total = jnp.concatenate([stat_ref[1:2, :], total], axis=1)
    own = rows // n_ctx
    part = own // reqs
    pairs = own // heads
    pair = part // heads
    to, frm = iota((rows, rows), 0), iota((rows, rows), 1)
    c, h, r, j = to // own, (to % own) // pairs, (to % pairs) // pair, to % pair
    perm = (frm == r * n_ctx * part + c * part + j * heads + h).astype(bf16)
    moved = dot(perm, sum_ref[...]).astype(bf16)
    fetch.wait()
    for c in range(n_ctx):
        for h in range(heads):
            lo = c * own + h * pairs
            value = dot(moved[lo : lo + pairs], up_ref[c, h])
            out_ref[c, h * pairs : (h + 1) * pairs, :] = value.astype(bf16)
    high = total.astype(bf16).astype(f32)
    line = iota((TABLE, rows), 0)
    packed = jnp.where(line == 0, top, 0.0)
    packed = jnp.where(line == 1, high, packed)
    packed = jnp.where(line == 2, total - high, packed)
    table = dot(packed.astype(bf16), perm, ((1,), (1,))).astype(bf16)
    for c in range(n_ctx):
        lo = c * own // LANES * LANES
        out_ref[c, own : own + TABLE, :] = table[:, lo : lo + LANES]


def merge_late(early, stats, arrived, value_up, count):
    n_ctx, heads, lat, vdim = value_up.shape
    rows = early.shape[0] + (arrived.shape[1] - TABLE) // (lat // LANES)
    return pl.pallas_call(
        functools.partial(merge_late_kernel, n_ctx, count),
        out_shape=jax.ShapeDtypeStruct((n_ctx, rows // n_ctx + TABLE, vdim), bf16),
        in_specs=[pl.BlockSpec(memory_space=pltpu.VMEM)] * 3 + [pl.BlockSpec(memory_space=pltpu.HBM)],
        scratch_shapes=[
            pltpu.VMEM((rows, lat), bf16),
            pltpu.VMEM((n_ctx, heads, lat, vdim), bf16),
            pltpu.SemaphoreType.DMA,
        ],
        compiler_params=pltpu.CompilerParams(vmem_limit_bytes=VMEM_LIMIT),
        name="merge_late",
    )(early, stats, arrived, in_hbm(value_up))


def project_kernel(place, in_ref, far_ref, out_ref, proj_ref, sum_ref, sems):
    sources, tall, vdim = in_ref.shape
    own = tall - TABLE
    blocks, rows, cols = out_ref.shape
    heads = own // rows
    copies = []
    for h in range(heads):
        part = pl.ds(h * vdim, vdim)
        copies.append(pltpu.make_async_copy(far_ref.at[part], proj_ref.at[part], sems.at[h]))
        copies[h].start()
    offset = lax.rem(place[0] * own, LANES)
    mine = (iota((own, LANES), 1) == offset + iota((own, LANES), 0)).astype(bf16)
    table = in_ref[:, own : own + TABLE, :]
    tops = dot(mine, table[:, 0, :], ((1,), (1,)))
    sums = dot(mine, table[:, 1, :], ((1,), (1,))) + dot(mine, table[:, 2, :], ((1,), (1,)))
    factor = jnp.exp2(tops - jnp.max(tops, axis=1, keepdims=True))
    total = jnp.sum(factor * sums, axis=1, keepdims=True)
    acc = jnp.zeros((own, vdim), f32)
    for s in range(sources):
        acc += in_ref[s, :own, :].astype(f32) * factor[:, s : s + 1]
    value = (acc / total).astype(bf16)
    for h in range(heads):
        copies[h].wait()
        for c in range(blocks):
            weight = proj_ref[h * vdim : (h + 1) * vdim, c * cols : (c + 1) * cols]
            term = dot(value[h * rows : (h + 1) * rows], weight)
            if h > 0:
                term += sum_ref[c]
            if h < heads - 1:
                sum_ref[c] = term
            else:
                out_ref[c] = term.astype(bf16)


def project(arrived, place, out_proj, n_ctx):
    sources, tall, vdim = arrived.shape
    depth, model = out_proj.shape
    cols = model // n_ctx
    rows = (tall - TABLE) * vdim // depth
    vmem = pl.BlockSpec(memory_space=pltpu.VMEM)
    return pl.pallas_call(
        project_kernel,
        out_shape=jax.ShapeDtypeStruct((n_ctx, rows, cols), bf16),
        in_specs=[pl.BlockSpec(memory_space=pltpu.SMEM), vmem, pl.BlockSpec(memory_space=pltpu.HBM)],
        out_specs=vmem,
        scratch_shapes=[
            pltpu.VMEM(out_proj.shape, bf16),
            pltpu.VMEM((n_ctx, rows, cols), f32),
            pltpu.SemaphoreType.DMA((depth // vdim,)),
        ],
        compiler_params=pltpu.CompilerParams(vmem_limit_bytes=VMEM_LIMIT),
        name="project",
    )(place, arrived, in_hbm(out_proj))


def expert_kernel(me, hid_ref, gain_ref, router_ref, routes_ref, gate_ref, *refs):
    far_refs, out_ref, (up_ref, down_ref, normed_ref, sems) = refs[:2], refs[2], refs[3:]
    blocks, rows, cols = hid_ref.shape
    experts = router_ref.shape[1]
    half_up, half_down = blocks // 2, down_ref.shape[0] // 2
    pieces = [(0, pl.ds(0, half_up)), (0, pl.ds(half_up, blocks - half_up))]
    pieces += [(1, pl.ds(0, half_down)), (1, pl.ds(half_down, half_down))]
    copies = [
        pltpu.make_async_copy(far_refs[n].at[piece], (up_ref, down_ref)[n].at[piece], sems.at[i])
        for i, (n, piece) in enumerate(pieces)
    ]
    for copy in copies:
        copy.start()
    square = jnp.zeros((rows, 1), f32)
    for c in range(blocks):
        h = hid_ref[c].astype(f32)
        square += jnp.sum(h * h, axis=1, keepdims=True)
    inverse = lax.rsqrt(square / (blocks * cols) + 1e-06)
    gate = jnp.zeros((rows, gate_ref.shape[2]), f32)
    up = jnp.zeros((rows, up_ref.shape[2]), f32)
    logits = jnp.zeros((rows, experts), f32)
    for c in range(blocks):
        normed = (hid_ref[c].astype(f32) * inverse * gain_ref[c].astype(f32)).astype(bf16)
        gate += dot(normed, gate_ref[c])
        logits += dot(normed, router_ref[c], ((1,), (1,)))
        normed_ref[c] = normed
    for c in range(blocks):
        if c == 0 or c == half_up:
            copies[c // half_up].wait()
        up += dot(normed_ref[c], up_ref[c])
    affinity = jax.nn.sigmoid(logits)
    lane = iota((rows, experts), 1)
    mine = jnp.zeros((rows, 1), f32)
    whole = jnp.zeros((rows, 1), f32)
    for k in range(routes_ref.shape[1]):
        choice = routes_ref[:, k : k + 1]
        picked = jnp.sum(jnp.where(lane == choice, affinity, 0.0), axis=1, keepdims=True)
        whole += picked
        mine += jnp.where(choice == me[0], picked, 0.0)
    weight = route_scale * mine / whole
    copies[2].wait()
    copies[3].wait()
    active = (gate / (1.0 + jnp.exp(-gate)) * up).astype(bf16)
    for c in range(blocks):
        got = dot(active, down_ref[:, c * cols : (c + 1) * cols])
        out_ref[c] = (got * weight).astype(bf16)


def experts_here(hidden, gain, router, routes, me, gate, up, down):
    vmem = pl.BlockSpec(memory_space=pltpu.VMEM)
    return pl.pallas_call(
        expert_kernel,
        out_shape=jax.ShapeDtypeStruct(hidden.shape, bf16),
        in_specs=[pl.BlockSpec(memory_space=pltpu.SMEM)]
        + [vmem] * 5
        + [pl.BlockSpec(memory_space=pltpu.HBM)] * 2,
        out_specs=vmem,
        scratch_shapes=[
            pltpu.VMEM(up.shape, bf16),
            pltpu.VMEM(down.shape, bf16),
            pltpu.VMEM(hidden.shape, bf16),
            pltpu.SemaphoreType.DMA((4,)),
        ],
        compiler_params=pltpu.CompilerParams(vmem_limit_bytes=VMEM_LIMIT),
        name="experts",
    )(me, hidden, gain, router, routes, gate, in_hbm(up), in_hbm(down))


def on_device(
    queries,
    latent_cache,
    context_lengths,
    value_up,
    out_proj,
    residual,
    norm_gain,
    router,
    routes,
    expert_gate,
    expert_up,
    expert_down,
):
    reqs, pair, heads, depth = queries.shape
    lat, vdim = value_up.shape[1:]
    scale = 1.0 / math.sqrt(vdim + depth - lat)
    n_ctx, n_exp = lax.axis_size("ctx"), lax.axis_size("exp")
    n_all = n_ctx * n_exp
    everyone = ("ctx", "exp")
    ctx, exp = lax.axis_index("ctx"), lax.axis_index("exp")
    own_rows, model = residual.shape
    top = routes.shape[1]
    cols = model // n_ctx
    experts = router.shape[1]

    def swap(x, axes):
        return lax.all_to_all(x, axes, split_axis=0, concat_axis=0, tiled=True)

    def spread(x, axes, size):
        return swap(jnp.broadcast_to(x[None], (size, *x.shape)), axes)

    early = reqs * 5 // 16
    counts = (early, reqs - early)
    per = pair * heads
    q = queries.reshape(reqs * per, depth)
    late = spread(q[early * per :], "exp", n_exp)
    late = late.reshape(n_exp, counts[1], per, depth).transpose(1, 0, 2, 3).reshape(counts[1], n_exp * per, depth)
    q, late = lax.optimization_barrier((q[: early * per], late))
    late = lax.all_gather(late, "ctx", axis=0)
    q = spread(q, "ctx", n_ctx)
    q = q.reshape(n_ctx, early, per, depth).transpose(1, 0, 2, 3).reshape(early * n_ctx * per, depth)
    q = spread(q, "exp", n_exp).reshape(n_exp, early, n_ctx * per, depth)

    base = ((ctx * n_exp + exp) * latent_cache.shape[1]).reshape(1)
    routes_row = jnp.zeros((1, LANES), f32).at[0, : own_rows * top].set(routes.reshape(-1).astype(f32))
    cache = in_hbm(latent_cache.swapaxes(1, 2))
    rest = (cache, context_lengths, base, routes_row, scale, n_ctx, n_exp, lat)
    sent = attend(q, *rest, 0, False)
    up, late = lax.optimization_barrier((value_up, late))
    all_up = lax.all_gather(up, "ctx", axis=0)
    late = in_hbm(late)
    arrived = swap(sent, "exp")
    sent, arrived = lax.optimization_barrier((attend(late, *rest, early, True), arrived))
    sums, stats, route_rows = merge_early(arrived, early, lat)
    all_routes = route_rows[:, : own_rows * top].astype(jnp.int32).reshape(n_exp, own_rows, top)
    sent, sums = lax.optimization_barrier((sent, sums))
    arrived = swap(sent, "exp")
    arrived = swap(merge_late(sums, stats, arrived, all_up, reqs - early), "ctx")
    terms = project(arrived, ctx.reshape(1), out_proj, n_ctx)

    terms = swap(terms.reshape(n_all, own_rows, cols), everyone)
    attention = jnp.sum(terms.astype(f32), axis=0)
    own = lax.dynamic_slice_in_dim(residual, ctx * cols, cols, 1)
    hidden = (own.astype(f32) + attention).astype(bf16)

    slots = max(2, own_rows * top // experts)
    before = jnp.tril(jnp.ones((own_rows, own_rows), jnp.int32), -1)

    def slot_of(named, axis):
        shape = (1,) * axis + (own_rows, own_rows) + (1,) * (named.ndim - 1 - axis)
        earlier = jnp.sum(before.reshape(shape) * jnp.expand_dims(named, axis), axis=axis + 1)
        return jnp.where(named == 1, earlier, -1)

    named = jnp.sum((routes[:, :, None] == jnp.arange(experts)).astype(jnp.int32), axis=1)
    place = (slot_of(named, 0)[:, :, None] == jnp.arange(slots)).astype(bf16)
    place = jnp.broadcast_to(place[:, None], (own_rows, n_ctx, experts, slots)).reshape(own_rows, -1)
    rows = dot(place, hidden, ((0,), (0,))).astype(bf16)
    rows = swap(rows.reshape(n_all, slots, cols), everyone)

    named = jnp.any(all_routes == exp, axis=2).astype(jnp.int32)
    taken = (slot_of(named, 1)[:, None, :] == jnp.arange(slots)[None, :, None]).astype(jnp.int32)
    slot_routes = jnp.sum(taken[..., None] * all_routes[:, None], axis=2).reshape(n_exp * slots, top)
    mixed = experts_here(
        rows.reshape(n_ctx, n_exp * slots, cols),
        norm_gain.reshape(n_ctx, 1, cols),
        router.T.reshape(experts, n_ctx, cols).transpose(1, 0, 2),
        slot_routes,
        exp.reshape(1),
        expert_gate.reshape(n_ctx, cols, -1),
        expert_up.reshape(n_ctx, cols, -1),
        expert_down[0],
    )
    mixed = swap(mixed.reshape(n_all, slots, cols), everyone)
    mixture = dot(place, mixed.reshape(n_all * slots, cols))
    return (hidden.astype(f32) + mixture).astype(bf16)


def solution(mesh):
    return jax.shard_map(
        on_device,
        mesh=mesh,
        in_specs=(
            P("req", None, ("ctx", "exp"), None),
            P("req", ("ctx", "exp"), None),
            P("req"),
            P(("ctx", "exp"), None, None),
            P(("ctx", "exp"), None),
            P(("req", "exp"), None),
            P(),
            P(),
            P(("req", "exp"), None),
            P("exp", None, "ctx"),
            P("exp", None, "ctx"),
            P("exp", "ctx", None),
        ),
        out_specs=P(("req", "exp"), "ctx"),
        check_vma=False,
    )
```

```python
import functools
import math

import jax
import jax.numpy as jnp
from jax import lax
from jax.experimental import pallas as pl
from jax.experimental.pallas import tpu as pltpu
from jax.sharding import PartitionSpec as P

route_scale = 2.5
f32 = jnp.float32
bf16 = jnp.bfloat16
VMEM_LIMIT = 16 * 1024 * 1024
LANES = 128
AHEAD = 4
LOG2E = math.log2(math.e)
TABLE = 16


def iota(shape, dim):
    return lax.broadcasted_iota(jnp.int32, shape, dim)


def dot(a, b, dims=((1,), (0,))):
    return lax.dot_general(a, b, (dims, ((), ())), preferred_element_type=f32)


def in_hbm(x):
    return pltpu.with_memory_space_constraint(x, pltpu.HBM)


def attend_kernel(scale, n_ctx, n_exp, first, permuted, steps, lengths, base, q_far, k_far, routes_ref, out_ref, *scratch):
    stat_ref, buf_ref, table_ref, sems, q_ref, k_ref, in_sems = scratch[:7]
    step = pl.program_id(0)
    slot = lax.rem(step, 2)
    ahead, n_outer, unroll, per, depth = q_ref.shape
    rows = n_outer * per
    chunk = rows // n_exp
    block = k_ref.shape[3]
    tall = out_ref.shape[1] - TABLE
    lines = stat_ref.shape[2] // LANES
    tiles = tall // (unroll * steps * chunk)
    width = tiles * LANES

    @pl.when(step == 0)
    def _():
        stat_ref[...] = jnp.zeros_like(stat_ref)
        if permuted:
            per_pair = rows // (n_ctx * n_exp)
            to, frm = iota((rows, rows), 0), iota((rows, rows), 1)
            e, c, rest = to // chunk, (to % chunk) // per_pair, to % per_pair
            scratch[7][...] = (frm == c * per + e * per_pair + rest).astype(bf16)

    def bring(where):
        into = lax.rem(where, ahead)
        mine, yours = pl.ds(where * unroll, unroll), pl.ds(first + where * unroll, unroll)
        return (
            pltpu.make_async_copy(q_far.at[:, mine], q_ref.at[into], in_sems.at[0, into]),
            pltpu.make_async_copy(k_far.at[yours], k_ref.at[into], in_sems.at[1, into]),
        )

    @pl.when(step == 0)
    def _():
        for where in range(min(ahead - 1, steps)):
            for copy in bring(where):
                copy.start()

    @pl.when(step + ahead - 1 < steps)
    def _():
        for copy in bring(step + ahead - 1):
            copy.start()

    for copy in bring(step):
        copy.wait()
    now = lax.rem(step, ahead)
    row = iota((rows, 1), 0)
    lane = iota((rows, block), 1)
    span = buf_ref.shape[2]

    def leave(which, where):
        place = out_ref.at[:, pl.ds(pl.multiple_of(where * span, span), span), :]
        return pltpu.make_async_copy(buf_ref.at[which], place, sems.at[which])

    @pl.when(step >= 2)
    def _():
        leave(slot, step - 2).wait()

    for u in range(unroll):
        r = step * unroll + u
        q = q_ref[now, :, u].reshape(rows, depth)
        if permuted:
            q = dot(scratch[7][...], q).astype(bf16)
        k = k_ref[now, u]
        scores = dot(q, k) * (scale * LOG2E)
        visible = lane < lengths[first + r] + (row // 2) % 2 - base[0]
        masked = jnp.where(visible, scores, -1e30)
        top = jnp.maximum(jnp.max(masked, axis=1, keepdims=True), -1e29).astype(bf16).astype(f32)
        weights = jnp.exp2(masked - top)
        total = jnp.sum(weights, axis=1, keepdims=True)
        got = dot(weights.astype(bf16), k[:width], ((1,), (1,)))
        got = got.astype(bf16).reshape(n_exp, chunk, width)
        for t in range(tiles):
            lo = (u * tiles + t) * chunk
            buf_ref[slot, :, lo : lo + chunk, :] = got[:, :, t * LANES : (t + 1) * LANES]
        spot = iota((chunk, lines * LANES), 1) == r * chunk + iota((chunk, lines * LANES), 0)
        spot = spot[None]
        stat_ref[0] += jnp.sum(jnp.where(spot, top.reshape(n_exp, chunk, 1), 0.0), axis=1)
        stat_ref[1] += jnp.sum(jnp.where(spot, total.reshape(n_exp, chunk, 1), 0.0), axis=1)

    leave(slot, step).start()

    @pl.when(step == steps - 1)
    def _():
        top, total = stat_ref[0], stat_ref[1]
        high = total.astype(bf16).astype(f32)
        line = iota((n_exp, TABLE, LANES), 1)
        table = jnp.where(line == TABLE - 1, routes_ref[...][None], 0.0)
        for kind, values in enumerate((top, high, total - high)):
            for w in range(lines):
                part = values[:, w * LANES : (w + 1) * LANES]
                table = jnp.where(line == kind * lines + w, part[:, None, :], table)
        table_ref[...] = table.astype(bf16)
        last = pltpu.make_async_copy(table_ref, out_ref.at[:, pl.ds(tall, TABLE), :], sems.at[2])
        last.start()

        @pl.when(step >= 1)
        def _():
            leave(1 - slot, step - 1).wait()

        leave(slot, step).wait()
        last.wait()


def attend(queries, cache, lengths, base, routes_row, scale, n_ctx, n_exp, lat, first, permuted):
    n_outer, reqs, per, depth = queries.shape
    block = cache.shape[2]
    rows = n_outer * per
    unroll = 2 if reqs % 2 == 0 and first % 2 == 0 else 1
    chunk = rows // n_exp
    tall = reqs * chunk * (lat // LANES) + TABLE
    wide = -(-reqs * chunk // LANES) * LANES
    return pl.pallas_call(
        functools.partial(attend_kernel, scale, n_ctx, n_exp, first, permuted, reqs // unroll),
        out_shape=pltpu.HBM((n_exp, tall, LANES), bf16),
        grid_spec=pltpu.PrefetchScalarGridSpec(
            num_scalar_prefetch=2,
            grid=(reqs // unroll,),
            in_specs=[
                pl.BlockSpec(memory_space=pl.ANY),
                pl.BlockSpec(memory_space=pl.ANY),
                pl.BlockSpec((1, LANES), lambda r, *_: (0, 0)),
            ],
            out_specs=pl.BlockSpec(memory_space=pltpu.HBM),
            scratch_shapes=[
                pltpu.VMEM((2, n_exp, wide), f32),
                pltpu.VMEM((2, n_exp, unroll * chunk * (lat // LANES), LANES), bf16),
                pltpu.VMEM((n_exp, TABLE, LANES), bf16),
                pltpu.SemaphoreType.DMA((3,)),
                pltpu.VMEM((AHEAD, n_outer, unroll, per, depth), bf16),
                pltpu.VMEM((AHEAD, unroll, depth, block), bf16),
                pltpu.SemaphoreType.DMA((2, AHEAD)),
            ]
            + ([pltpu.VMEM((rows, rows), bf16)] if permuted else []),
        ),
        compiler_params=pltpu.CompilerParams(vmem_limit_bytes=VMEM_LIMIT),
        cost_estimate=pl.CostEstimate(
            flops=4 * reqs * rows * block * depth,
            bytes_accessed=2 * reqs * (depth * block + rows * (depth + lat)),
            transcendentals=reqs * rows * block,
        ),
        name="attend",
    )(lengths, base, queries, cache, routes_row)


def merge_rows(in_ref, sum_ref, first, count):
    sources, tall, _ = in_ref.shape
    tall -= TABLE
    tiles = sum_ref.shape[1] // LANES
    chunk = tall // (count * tiles)
    lines = -(-count * chunk // LANES)
    table = in_ref[:, tall : tall + TABLE, :].astype(f32)

    def kind(n):
        return jnp.concatenate([table[:, n * lines + w, :] for w in range(lines)], axis=1)

    tops, sums = kind(0), kind(1) + kind(2)
    top = jnp.max(tops, axis=0, keepdims=True)
    factor = jnp.exp2(tops - top)
    columns = factor.T
    for r in range(count):
        lo = r * chunk
        for t in range(tiles):
            acc = jnp.zeros((chunk, LANES), f32)
            for s in range(sources):
                at = (r * tiles + t) * chunk
                acc += in_ref[s, at : at + chunk, :].astype(f32) * columns[lo : lo + chunk, s : s + 1]
            sum_ref[first + lo : first + lo + chunk, t * LANES : (t + 1) * LANES] = acc.astype(bf16)
    total = jnp.sum(factor * sums, axis=0, keepdims=True)
    return top[:, : count * chunk], total[:, : count * chunk], table[:, TABLE - 1, :]


def merge_early_kernel(count, in_ref, sum_ref, stat_ref, routes_ref):
    top, total, routes_ref[...] = merge_rows(in_ref, sum_ref, 0, count)
    line = iota(stat_ref.shape, 0)
    stat_ref[...] = jnp.where(line == 0, top, jnp.where(line == 1, total, 0.0))


def merge_early(arrived, count, lat):
    sources, tall, _ = arrived.shape
    rows = (tall - TABLE) // (lat // LANES)
    return pl.pallas_call(
        functools.partial(merge_early_kernel, count),
        out_shape=(
            jax.ShapeDtypeStruct((rows, lat), bf16),
            jax.ShapeDtypeStruct((8, rows), f32),
            jax.ShapeDtypeStruct((sources, LANES), f32),
        ),
        compiler_params=pltpu.CompilerParams(vmem_limit_bytes=VMEM_LIMIT),
        cost_estimate=pl.CostEstimate(
            flops=4 * arrived.size, bytes_accessed=2 * arrived.size, transcendentals=sources * rows
        ),
        name="merge_early",
    )(arrived)


def merge_late_kernel(n_ctx, count, early_ref, stat_ref, in_ref, far_ref, out_ref, sum_ref, up_ref, sem):
    rows, lat = sum_ref.shape
    first = early_ref.shape[0]
    fetch = pltpu.make_async_copy(far_ref, up_ref, sem)
    fetch.start()
    heads = up_ref.shape[1]
    reqs = count * rows // (rows - first)
    sum_ref[:first, :] = early_ref[...]
    top, total, _ = merge_rows(in_ref, sum_ref, first, count)
    top = jnp.concatenate([stat_ref[0:1, :], top], axis=1)
    total = jnp.concatenate([stat_ref[1:2, :], total], axis=1)
    own = rows // n_ctx
    part = own // reqs
    pairs = own // heads
    pair = part // heads
    to, frm = iota((rows, rows), 0), iota((rows, rows), 1)
    c, h, r, j = to // own, (to % own) // pairs, (to % pairs) // pair, to % pair
    perm = (frm == r * n_ctx * part + c * part + j * heads + h).astype(bf16)
    moved = dot(perm, sum_ref[...]).astype(bf16)
    fetch.wait()
    for c in range(n_ctx):
        for h in range(heads):
            lo = c * own + h * pairs
            value = dot(moved[lo : lo + pairs], up_ref[c, h])
            out_ref[c, h * pairs : (h + 1) * pairs, :] = value.astype(bf16)
    high = total.astype(bf16).astype(f32)
    line = iota((TABLE, rows), 0)
    packed = jnp.where(line == 0, top, 0.0)
    packed = jnp.where(line == 1, high, packed)
    packed = jnp.where(line == 2, total - high, packed)
    table = dot(packed.astype(bf16), perm, ((1,), (1,))).astype(bf16)
    for c in range(n_ctx):
        lo = c * own // LANES * LANES
        out_ref[c, own : own + TABLE, :] = table[:, lo : lo + LANES]


def merge_late(early, stats, arrived, value_up, count):
    n_ctx, heads, lat, vdim = value_up.shape
    rows = early.shape[0] + (arrived.shape[1] - TABLE) // (lat // LANES)
    return pl.pallas_call(
        functools.partial(merge_late_kernel, n_ctx, count),
        out_shape=jax.ShapeDtypeStruct((n_ctx, rows // n_ctx + TABLE, vdim), bf16),
        in_specs=[pl.BlockSpec(memory_space=pltpu.VMEM)] * 3 + [pl.BlockSpec(memory_space=pltpu.HBM)],
        scratch_shapes=[
            pltpu.VMEM((rows, lat), bf16),
            pltpu.VMEM((n_ctx, heads, lat, vdim), bf16),
            pltpu.SemaphoreType.DMA,
        ],
        compiler_params=pltpu.CompilerParams(vmem_limit_bytes=VMEM_LIMIT),
        name="merge_late",
    )(early, stats, arrived, in_hbm(value_up))


def project_kernel(place, in_ref, far_ref, out_ref, proj_ref, sum_ref, sems):
    sources, tall, vdim = in_ref.shape
    own = tall - TABLE
    blocks, rows, cols = sum_ref.shape
    each = out_ref.shape[0] // blocks
    heads = own // rows
    copies = []
    for h in range(heads):
        part = pl.ds(h * vdim, vdim)
        copies.append(pltpu.make_async_copy(far_ref.at[part], proj_ref.at[part], sems.at[h]))
        copies[h].start()
    offset = lax.rem(place[0] * own, LANES)
    mine = (iota((own, LANES), 1) == offset + iota((own, LANES), 0)).astype(bf16)
    table = in_ref[:, own : own + TABLE, :]
    tops = dot(mine, table[:, 0, :], ((1,), (1,)))
    sums = dot(mine, table[:, 1, :], ((1,), (1,))) + dot(mine, table[:, 2, :], ((1,), (1,)))
    factor = jnp.exp2(tops - jnp.max(tops, axis=1, keepdims=True))
    total = jnp.sum(factor * sums, axis=1, keepdims=True)
    acc = jnp.zeros((own, vdim), f32)
    for s in range(sources):
        acc += in_ref[s, :own, :].astype(f32) * factor[:, s : s + 1]
    value = (acc / total).astype(bf16)
    for h in range(heads):
        copies[h].wait()
        for c in range(blocks):
            weight = proj_ref[h * vdim : (h + 1) * vdim, c * cols : (c + 1) * cols]
            term = dot(value[h * rows : (h + 1) * rows], weight)
            if h > 0:
                term += sum_ref[c]
            if h < heads - 1:
                sum_ref[c] = term
            else:
                out_ref[c * each : (c + 1) * each] = term.reshape(each, rows // each, cols).astype(bf16)


def project(arrived, place, out_proj, n_ctx, n_exp):
    sources, tall, vdim = arrived.shape
    depth, model = out_proj.shape
    cols = model // n_ctx
    rows = (tall - TABLE) * vdim // depth
    shape = (n_ctx * n_exp, rows // n_exp, cols)
    vmem = pl.BlockSpec(memory_space=pltpu.VMEM)
    return pl.pallas_call(
        project_kernel,
        out_shape=pltpu.HBM(shape, bf16),
        in_specs=[pl.BlockSpec(memory_space=pltpu.SMEM), vmem, pl.BlockSpec(memory_space=pltpu.HBM)],
        out_specs=pl.BlockSpec(shape, lambda: (0, 0, 0)),
        scratch_shapes=[
            pltpu.VMEM(out_proj.shape, bf16),
            pltpu.VMEM((n_ctx, rows, cols), f32),
            pltpu.SemaphoreType.DMA((depth // vdim,)),
        ],
        compiler_params=pltpu.CompilerParams(vmem_limit_bytes=VMEM_LIMIT),
        name="project",
    )(place, arrived, in_hbm(out_proj))


def expert_kernel(me, hid_ref, gain_ref, router_ref, routes_ref, gate_ref, *refs):
    far_refs, out_ref, (up_ref, down_ref, normed_ref, sems) = refs[:2], refs[2], refs[3:]
    blocks, rows, cols = hid_ref.shape
    experts = router_ref.shape[1]
    half_up, half_down = blocks // 2, down_ref.shape[0] // 2
    pieces = [(0, pl.ds(0, half_up)), (0, pl.ds(half_up, blocks - half_up))]
    pieces += [(1, pl.ds(0, half_down)), (1, pl.ds(half_down, half_down))]
    copies = [
        pltpu.make_async_copy(far_refs[n].at[piece], (up_ref, down_ref)[n].at[piece], sems.at[i])
        for i, (n, piece) in enumerate(pieces)
    ]
    for copy in copies:
        copy.start()
    square = jnp.zeros((rows, 1), f32)
    for c in range(blocks):
        h = hid_ref[c].astype(f32)
        square += jnp.sum(h * h, axis=1, keepdims=True)
    inverse = lax.rsqrt(square / (blocks * cols) + 1e-06)
    gate = jnp.zeros((rows, gate_ref.shape[2]), f32)
    up = jnp.zeros((rows, up_ref.shape[2]), f32)
    logits = jnp.zeros((rows, experts), f32)
    for c in range(blocks):
        normed = (hid_ref[c].astype(f32) * inverse * gain_ref[c].astype(f32)).astype(bf16)
        gate += dot(normed, gate_ref[c])
        logits += dot(normed, router_ref[c], ((1,), (1,)))
        normed_ref[c] = normed
    for c in range(blocks):
        if c == 0 or c == half_up:
            copies[c // half_up].wait()
        up += dot(normed_ref[c], up_ref[c])
    affinity = jax.nn.sigmoid(logits)
    lane = iota((rows, experts), 1)
    mine = jnp.zeros((rows, 1), f32)
    whole = jnp.zeros((rows, 1), f32)
    for k in range(routes_ref.shape[1]):
        choice = routes_ref[:, k : k + 1]
        picked = jnp.sum(jnp.where(lane == choice, affinity, 0.0), axis=1, keepdims=True)
        whole += picked
        mine += jnp.where(choice == me[0], picked, 0.0)
    weight = route_scale * mine / whole
    copies[2].wait()
    copies[3].wait()
    active = (gate / (1.0 + jnp.exp(-gate)) * up).astype(bf16)
    for c in range(blocks):
        got = dot(active, down_ref[:, c * cols : (c + 1) * cols])
        out_ref[c] = (got * weight).astype(bf16)


def experts_here(hidden, gain, router, routes, me, gate, up, down):
    vmem = pl.BlockSpec(memory_space=pltpu.VMEM)
    return pl.pallas_call(
        expert_kernel,
        out_shape=jax.ShapeDtypeStruct(hidden.shape, bf16),
        in_specs=[pl.BlockSpec(memory_space=pltpu.SMEM)]
        + [vmem] * 5
        + [pl.BlockSpec(memory_space=pltpu.HBM)] * 2,
        out_specs=vmem,
        scratch_shapes=[
            pltpu.VMEM(up.shape, bf16),
            pltpu.VMEM(down.shape, bf16),
            pltpu.VMEM(hidden.shape, bf16),
            pltpu.SemaphoreType.DMA((4,)),
        ],
        compiler_params=pltpu.CompilerParams(vmem_limit_bytes=VMEM_LIMIT),
        name="experts",
    )(me, hidden, gain, router, routes, gate, in_hbm(up), in_hbm(down))


def on_device(
    queries,
    latent_cache,
    context_lengths,
    value_up,
    out_proj,
    residual,
    norm_gain,
    router,
    routes,
    expert_gate,
    expert_up,
    expert_down,
):
    reqs, pair, heads, depth = queries.shape
    lat, vdim = value_up.shape[1:]
    scale = 1.0 / math.sqrt(vdim + depth - lat)
    n_ctx, n_exp = lax.axis_size("ctx"), lax.axis_size("exp")
    n_all = n_ctx * n_exp
    everyone = ("ctx", "exp")
    ctx, exp = lax.axis_index("ctx"), lax.axis_index("exp")
    own_rows, model = residual.shape
    top = routes.shape[1]
    cols = model // n_ctx
    experts = router.shape[1]

    def swap(x, axes):
        return lax.all_to_all(x, axes, split_axis=0, concat_axis=0, tiled=True)

    def spread(x, axes, size):
        return swap(jnp.broadcast_to(x[None], (size, *x.shape)), axes)

    early = reqs * 5 // 16
    counts = (early, reqs - early)
    per = pair * heads
    q = queries.reshape(reqs * per, depth)
    late = spread(q[early * per :], "exp", n_exp)
    late = late.reshape(n_exp, counts[1], per, depth).transpose(1, 0, 2, 3).reshape(counts[1], n_exp * per, depth)
    q, late = lax.optimization_barrier((q[: early * per], late))
    late = lax.all_gather(late, "ctx", axis=0)
    q = spread(q, "ctx", n_ctx)
    q = q.reshape(n_ctx, early, per, depth).transpose(1, 0, 2, 3).reshape(early * n_ctx * per, depth)
    q = spread(q, "exp", n_exp).reshape(n_exp, early, n_ctx * per, depth)

    base = ((ctx * n_exp + exp) * latent_cache.shape[1]).reshape(1)
    routes_row = jnp.zeros((1, LANES), f32).at[0, : own_rows * top].set(routes.reshape(-1).astype(f32))
    cache = in_hbm(latent_cache.swapaxes(1, 2))
    rest = (cache, context_lengths, base, routes_row, scale, n_ctx, n_exp, lat)
    sent = attend(q, *rest, 0, False)
    up, late = lax.optimization_barrier((value_up, late))
    all_up = lax.all_gather(up, "ctx", axis=0)
    late = in_hbm(late)
    arrived = swap(sent, "exp")
    sent, arrived = lax.optimization_barrier((attend(late, *rest, early, True), arrived))
    sums, stats, route_rows = merge_early(arrived, early, lat)
    all_routes = route_rows[:, : own_rows * top].astype(jnp.int32).reshape(n_exp, own_rows, top)
    sent, sums = lax.optimization_barrier((sent, sums))
    arrived = swap(sent, "exp")
    arrived = swap(merge_late(sums, stats, arrived, all_up, reqs - early), "ctx")
    own = lax.dynamic_slice_in_dim(residual, ctx * cols, cols, 1).astype(f32)
    arrived, own = lax.optimization_barrier((arrived, own))
    terms = project(arrived, ctx.reshape(1), out_proj, n_ctx, n_exp)

    terms = swap(terms, everyone)
    attention = jnp.sum(terms.astype(f32), axis=0)
    hidden = (own + attention).astype(bf16)

    slots = max(2, own_rows * top // experts)
    before = jnp.tril(jnp.ones((own_rows, own_rows), jnp.int32), -1)

    def slot_of(named, axis):
        shape = (1,) * axis + (own_rows, own_rows) + (1,) * (named.ndim - 1 - axis)
        earlier = jnp.sum(before.reshape(shape) * jnp.expand_dims(named, axis), axis=axis + 1)
        return jnp.where(named == 1, earlier, -1)

    named = jnp.sum((routes[:, :, None] == jnp.arange(experts)).astype(jnp.int32), axis=1)
    place = (slot_of(named, 0)[:, :, None] == jnp.arange(slots)).astype(bf16)
    place = jnp.broadcast_to(place[:, None], (own_rows, n_ctx, experts, slots)).reshape(own_rows, -1)
    rows = dot(place, hidden, ((0,), (0,))).astype(bf16)
    rows = swap(rows.reshape(n_all, slots, cols), everyone)

    named = jnp.any(all_routes == exp, axis=2).astype(jnp.int32)
    taken = (slot_of(named, 1)[:, None, :] == jnp.arange(slots)[None, :, None]).astype(jnp.int32)
    slot_routes = jnp.sum(taken[..., None] * all_routes[:, None], axis=2).reshape(n_exp * slots, top)
    mixed = experts_here(
        rows.reshape(n_ctx, n_exp * slots, cols),
        norm_gain.reshape(n_ctx, 1, cols),
        router.T.reshape(experts, n_ctx, cols).transpose(1, 0, 2),
        slot_routes,
        exp.reshape(1),
        expert_gate.reshape(n_ctx, cols, -1),
        expert_up.reshape(n_ctx, cols, -1),
        expert_down[0],
    )
    mixed = swap(mixed.reshape(n_all, slots, cols), everyone)
    mixture = dot(place, mixed.reshape(n_all * slots, cols))
    return (hidden.astype(f32) + mixture).astype(bf16)


def solution(mesh):
    return jax.shard_map(
        on_device,
        mesh=mesh,
        in_specs=(
            P("req", None, ("ctx", "exp"), None),
            P("req", ("ctx", "exp"), None),
            P("req"),
            P(("ctx", "exp"), None, None),
            P(("ctx", "exp"), None),
            P(("req", "exp"), None),
            P(),
            P(),
            P(("req", "exp"), None),
            P("exp", None, "ctx"),
            P("exp", None, "ctx"),
            P("exp", "ctx", None),
        ),
        out_specs=P(("req", "exp"), "ctx"),
        check_vma=False,
    )
```

```python
import functools
import math

import jax
import jax.numpy as jnp
from jax import lax
from jax.experimental import pallas as pl
from jax.experimental.pallas import tpu as pltpu
from jax.sharding import PartitionSpec as P

route_scale = 2.5
f32 = jnp.float32
bf16 = jnp.bfloat16
VMEM_LIMIT = 16 * 1024 * 1024
LANES = 128
AHEAD = 4
LOG2E = math.log2(math.e)
TABLE = 16


def iota(shape, dim):
    return lax.broadcasted_iota(jnp.int32, shape, dim)


def dot(a, b, dims=((1,), (0,))):
    return lax.dot_general(a, b, (dims, ((), ())), preferred_element_type=f32)


def in_hbm(x):
    return pltpu.with_memory_space_constraint(x, pltpu.HBM)


def attend_kernel(scale, n_ctx, n_exp, first, permuted, steps, lengths, base, q_far, k_far, routes_ref, out_ref, *scratch):
    stat_ref, buf_ref, table_ref, sems, q_ref, k_ref, in_sems = scratch[:7]
    step = pl.program_id(0)
    slot = lax.rem(step, 2)
    ahead, n_outer, unroll, per, depth = q_ref.shape
    rows = n_outer * per
    chunk = rows // n_exp
    block = k_ref.shape[3]
    tall = out_ref.shape[1] - TABLE
    lines = stat_ref.shape[2] // LANES
    tiles = tall // (unroll * steps * chunk)
    width = tiles * LANES

    @pl.when(step == 0)
    def _():
        stat_ref[...] = jnp.zeros_like(stat_ref)
        if permuted:
            per_pair = rows // (n_ctx * n_exp)
            to, frm = iota((rows, rows), 0), iota((rows, rows), 1)
            e, c, rest = to // chunk, (to % chunk) // per_pair, to % per_pair
            scratch[7][...] = (frm == c * per + e * per_pair + rest).astype(bf16)

    def bring(where):
        into = lax.rem(where, ahead)
        mine, yours = pl.ds(where * unroll, unroll), pl.ds(first + where * unroll, unroll)
        return (
            pltpu.make_async_copy(q_far.at[:, mine], q_ref.at[into], in_sems.at[0, into]),
            pltpu.make_async_copy(k_far.at[yours], k_ref.at[into], in_sems.at[1, into]),
        )

    @pl.when(step == 0)
    def _():
        for where in range(min(ahead - 1, steps)):
            for copy in bring(where):
                copy.start()

    @pl.when(step + ahead - 1 < steps)
    def _():
        for copy in bring(step + ahead - 1):
            copy.start()

    for copy in bring(step):
        copy.wait()
    now = lax.rem(step, ahead)
    row = iota((rows, 1), 0)
    lane = iota((rows, block), 1)
    span = buf_ref.shape[2]

    def leave(which, where):
        place = out_ref.at[:, pl.ds(pl.multiple_of(where * span, span), span), :]
        return pltpu.make_async_copy(buf_ref.at[which], place, sems.at[which])

    @pl.when(step >= 2)
    def _():
        leave(slot, step - 2).wait()

    for u in range(unroll):
        r = step * unroll + u
        q = q_ref[now, :, u].reshape(rows, depth)
        if permuted:
            q = dot(scratch[7][...], q).astype(bf16)
        k = k_ref[now, u]
        scores = dot(q, k) * (scale * LOG2E)
        visible = lane < lengths[first + r] + (row // 2) % 2 - base[0]
        masked = jnp.where(visible, scores, -1e30)
        top = jnp.maximum(jnp.max(masked, axis=1, keepdims=True), -1e29).astype(bf16).astype(f32)
        weights = jnp.exp2(masked - top)
        total = jnp.sum(weights, axis=1, keepdims=True)
        got = dot(weights.astype(bf16), k[:width], ((1,), (1,)))
        got = got.astype(bf16).reshape(n_exp, chunk, width)
        for t in range(tiles):
            lo = (u * tiles + t) * chunk
            buf_ref[slot, :, lo : lo + chunk, :] = got[:, :, t * LANES : (t + 1) * LANES]
        spot = iota((chunk, lines * LANES), 1) == r * chunk + iota((chunk, lines * LANES), 0)
        spot = spot[None]
        stat_ref[0] += jnp.sum(jnp.where(spot, top.reshape(n_exp, chunk, 1), 0.0), axis=1)
        stat_ref[1] += jnp.sum(jnp.where(spot, total.reshape(n_exp, chunk, 1), 0.0), axis=1)

    leave(slot, step).start()

    @pl.when(step == steps - 1)
    def _():
        top, total = stat_ref[0], stat_ref[1]
        high = total.astype(bf16).astype(f32)
        line = iota((n_exp, TABLE, LANES), 1)
        table = jnp.where(line == TABLE - 1, routes_ref[...][None], 0.0)
        for kind, values in enumerate((top, high, total - high)):
            for w in range(lines):
                part = values[:, w * LANES : (w + 1) * LANES]
                table = jnp.where(line == kind * lines + w, part[:, None, :], table)
        table_ref[...] = table.astype(bf16)
        last = pltpu.make_async_copy(table_ref, out_ref.at[:, pl.ds(tall, TABLE), :], sems.at[2])
        last.start()

        @pl.when(step >= 1)
        def _():
            leave(1 - slot, step - 1).wait()

        leave(slot, step).wait()
        last.wait()


def attend(queries, cache, lengths, base, routes_row, scale, n_ctx, n_exp, lat, first, permuted):
    n_outer, reqs, per, depth = queries.shape
    block = cache.shape[2]
    rows = n_outer * per
    unroll = 2 if reqs % 2 == 0 and first % 2 == 0 else 1
    chunk = rows // n_exp
    tall = reqs * chunk * (lat // LANES) + TABLE
    wide = -(-reqs * chunk // LANES) * LANES
    return pl.pallas_call(
        functools.partial(attend_kernel, scale, n_ctx, n_exp, first, permuted, reqs // unroll),
        out_shape=pltpu.HBM((n_exp, tall, LANES), bf16),
        grid_spec=pltpu.PrefetchScalarGridSpec(
            num_scalar_prefetch=2,
            grid=(reqs // unroll,),
            in_specs=[
                pl.BlockSpec(memory_space=pl.ANY),
                pl.BlockSpec(memory_space=pl.ANY),
                pl.BlockSpec((1, LANES), lambda r, *_: (0, 0)),
            ],
            out_specs=pl.BlockSpec(memory_space=pltpu.HBM),
            scratch_shapes=[
                pltpu.VMEM((2, n_exp, wide), f32),
                pltpu.VMEM((2, n_exp, unroll * chunk * (lat // LANES), LANES), bf16),
                pltpu.VMEM((n_exp, TABLE, LANES), bf16),
                pltpu.SemaphoreType.DMA((3,)),
                pltpu.VMEM((AHEAD, n_outer, unroll, per, depth), bf16),
                pltpu.VMEM((AHEAD, unroll, depth, block), bf16),
                pltpu.SemaphoreType.DMA((2, AHEAD)),
            ]
            + ([pltpu.VMEM((rows, rows), bf16)] if permuted else []),
        ),
        compiler_params=pltpu.CompilerParams(vmem_limit_bytes=VMEM_LIMIT),
        cost_estimate=pl.CostEstimate(
            flops=4 * reqs * rows * block * depth,
            bytes_accessed=2 * reqs * (depth * block + rows * (depth + lat)),
            transcendentals=reqs * rows * block,
        ),
        name="attend",
    )(lengths, base, queries, cache, routes_row)


def merge_rows(in_ref, sum_ref, first, count):
    sources, tall, _ = in_ref.shape
    tall -= TABLE
    tiles = sum_ref.shape[1] // LANES
    chunk = tall // (count * tiles)
    lines = -(-count * chunk // LANES)
    table = in_ref[:, tall : tall + TABLE, :].astype(f32)

    def kind(n):
        return jnp.concatenate([table[:, n * lines + w, :] for w in range(lines)], axis=1)

    tops, sums = kind(0), kind(1) + kind(2)
    top = jnp.max(tops, axis=0, keepdims=True)
    factor = jnp.exp2(tops - top)
    columns = factor.T
    for r in range(count):
        lo = r * chunk
        for t in range(tiles):
            acc = jnp.zeros((chunk, LANES), f32)
            for s in range(sources):
                at = (r * tiles + t) * chunk
                acc += in_ref[s, at : at + chunk, :].astype(f32) * columns[lo : lo + chunk, s : s + 1]
            sum_ref[first + lo : first + lo + chunk, t * LANES : (t + 1) * LANES] = acc.astype(bf16)
    total = jnp.sum(factor * sums, axis=0, keepdims=True)
    return top[:, : count * chunk], total[:, : count * chunk], table[:, TABLE - 1, :]


def merge_early_kernel(count, in_ref, sum_ref, stat_ref, routes_ref):
    top, total, routes_ref[...] = merge_rows(in_ref, sum_ref, 0, count)
    line = iota(stat_ref.shape, 0)
    stat_ref[...] = jnp.where(line == 0, top, jnp.where(line == 1, total, 0.0))


def merge_early(arrived, count, lat):
    sources, tall, _ = arrived.shape
    rows = (tall - TABLE) // (lat // LANES)
    return pl.pallas_call(
        functools.partial(merge_early_kernel, count),
        out_shape=(
            jax.ShapeDtypeStruct((rows, lat), bf16),
            jax.ShapeDtypeStruct((8, rows), f32),
            jax.ShapeDtypeStruct((sources, LANES), f32),
        ),
        compiler_params=pltpu.CompilerParams(vmem_limit_bytes=VMEM_LIMIT),
        cost_estimate=pl.CostEstimate(
            flops=4 * arrived.size, bytes_accessed=2 * arrived.size, transcendentals=sources * rows
        ),
        name="merge_early",
    )(arrived)


def merge_late_kernel(n_ctx, count, early_ref, stat_ref, in_ref, far_ref, out_ref, sum_ref, up_ref, sem):
    rows, lat = sum_ref.shape
    first = early_ref.shape[0]
    fetch = pltpu.make_async_copy(far_ref, up_ref, sem)
    fetch.start()
    heads = up_ref.shape[1]
    reqs = count * rows // (rows - first)
    sum_ref[:first, :] = early_ref[...]
    top, total, _ = merge_rows(in_ref, sum_ref, first, count)
    top = jnp.concatenate([stat_ref[0:1, :], top], axis=1)
    total = jnp.concatenate([stat_ref[1:2, :], total], axis=1)
    own = rows // n_ctx
    part = own // reqs
    pairs = own // heads
    pair = part // heads
    to, frm = iota((rows, rows), 0), iota((rows, rows), 1)
    c, h, r, j = to // own, (to % own) // pairs, (to % pairs) // pair, to % pair
    perm = (frm == r * n_ctx * part + c * part + j * heads + h).astype(bf16)
    moved = dot(perm, sum_ref[...]).astype(bf16)
    fetch.wait()
    for c in range(n_ctx):
        for h in range(heads):
            lo = c * own + h * pairs
            value = dot(moved[lo : lo + pairs], up_ref[c, h])
            out_ref[c, h * pairs : (h + 1) * pairs, :] = value.astype(bf16)
    high = total.astype(bf16).astype(f32)
    line = iota((TABLE, rows), 0)
    packed = jnp.where(line == 0, top, 0.0)
    packed = jnp.where(line == 1, high, packed)
    packed = jnp.where(line == 2, total - high, packed)
    table = dot(packed.astype(bf16), perm, ((1,), (1,))).astype(bf16)
    for c in range(n_ctx):
        lo = c * own // LANES * LANES
        out_ref[c, own : own + TABLE, :] = table[:, lo : lo + LANES]


def merge_late(early, stats, arrived, value_up, count):
    n_ctx, heads, lat, vdim = value_up.shape
    rows = early.shape[0] + (arrived.shape[1] - TABLE) // (lat // LANES)
    return pl.pallas_call(
        functools.partial(merge_late_kernel, n_ctx, count),
        out_shape=jax.ShapeDtypeStruct((n_ctx, rows // n_ctx + TABLE, vdim), bf16),
        in_specs=[pl.BlockSpec(memory_space=pltpu.VMEM)] * 3 + [pl.BlockSpec(memory_space=pltpu.HBM)],
        scratch_shapes=[
            pltpu.VMEM((rows, lat), bf16),
            pltpu.VMEM((n_ctx, heads, lat, vdim), bf16),
            pltpu.SemaphoreType.DMA,
        ],
        compiler_params=pltpu.CompilerParams(vmem_limit_bytes=VMEM_LIMIT),
        name="merge_late",
    )(early, stats, arrived, in_hbm(value_up))


def project_kernel(place, in_ref, far_ref, out_ref, proj_ref, sum_ref, sems):
    sources, tall, vdim = in_ref.shape
    own = tall - TABLE
    blocks, rows, cols = sum_ref.shape
    each = out_ref.shape[0] // blocks
    heads = own // rows
    copies = []
    for h in range(heads):
        part = pl.ds(h * vdim, vdim)
        copies.append(pltpu.make_async_copy(far_ref.at[part], proj_ref.at[part], sems.at[h]))
        copies[h].start()
    offset = lax.rem(place[0] * own, LANES)
    mine = (iota((own, LANES), 1) == offset + iota((own, LANES), 0)).astype(bf16)
    table = in_ref[:, own : own + TABLE, :]
    tops = dot(mine, table[:, 0, :], ((1,), (1,)))
    sums = dot(mine, table[:, 1, :], ((1,), (1,))) + dot(mine, table[:, 2, :], ((1,), (1,)))
    factor = jnp.exp2(tops - jnp.max(tops, axis=1, keepdims=True))
    total = jnp.sum(factor * sums, axis=1, keepdims=True)
    acc = jnp.zeros((own, vdim), f32)
    for s in range(sources):
        acc += in_ref[s, :own, :].astype(f32) * factor[:, s : s + 1]
    value = (acc / total).astype(bf16)
    for h in range(heads):
        copies[h].wait()
        for c in range(blocks):
            weight = proj_ref[h * vdim : (h + 1) * vdim, c * cols : (c + 1) * cols]
            term = dot(value[h * rows : (h + 1) * rows], weight)
            if h > 0:
                term += sum_ref[c]
            if h < heads - 1:
                sum_ref[c] = term
            else:
                out_ref[c * each : (c + 1) * each] = term.reshape(each, rows // each, cols).astype(bf16)


def project(arrived, place, out_proj, n_ctx, n_exp):
    sources, tall, vdim = arrived.shape
    depth, model = out_proj.shape
    cols = model // n_ctx
    rows = (tall - TABLE) * vdim // depth
    shape = (n_ctx * n_exp, rows // n_exp, cols)
    vmem = pl.BlockSpec(memory_space=pltpu.VMEM)
    return pl.pallas_call(
        project_kernel,
        out_shape=pltpu.HBM(shape, bf16),
        in_specs=[pl.BlockSpec(memory_space=pltpu.SMEM), vmem, pl.BlockSpec(memory_space=pltpu.HBM)],
        out_specs=pl.BlockSpec(shape, lambda: (0, 0, 0)),
        scratch_shapes=[
            pltpu.VMEM(out_proj.shape, bf16),
            pltpu.VMEM((n_ctx, rows, cols), f32),
            pltpu.SemaphoreType.DMA((depth // vdim,)),
        ],
        compiler_params=pltpu.CompilerParams(vmem_limit_bytes=VMEM_LIMIT),
        name="project",
    )(place, arrived, in_hbm(out_proj))


def expert_kernel(me, hid_ref, gain_ref, router_ref, routes_ref, gate_ref, *refs):
    far_refs, out_ref, (up_ref, down_ref, normed_ref, sems) = refs[:2], refs[2], refs[3:]
    blocks, rows, cols = hid_ref.shape
    experts = router_ref.shape[1]
    half_up, half_down = blocks // 2, down_ref.shape[0] // 2
    pieces = [(0, pl.ds(0, half_up)), (0, pl.ds(half_up, blocks - half_up))]
    pieces += [(1, pl.ds(0, half_down)), (1, pl.ds(half_down, half_down))]
    copies = [
        pltpu.make_async_copy(far_refs[n].at[piece], (up_ref, down_ref)[n].at[piece], sems.at[i])
        for i, (n, piece) in enumerate(pieces)
    ]
    for copy in copies:
        copy.start()
    square = jnp.zeros((rows, 1), f32)
    for c in range(blocks):
        h = hid_ref[c].astype(f32)
        square += jnp.sum(h * h, axis=1, keepdims=True)
    inverse = lax.rsqrt(square / (blocks * cols) + 1e-06)
    gate = jnp.zeros((rows, gate_ref.shape[2]), f32)
    up = jnp.zeros((rows, up_ref.shape[2]), f32)
    logits = jnp.zeros((rows, experts), f32)
    for c in range(blocks):
        normed = (hid_ref[c].astype(f32) * inverse * gain_ref[c].astype(f32)).astype(bf16)
        gate += dot(normed, gate_ref[c])
        logits += dot(normed, router_ref[c], ((1,), (1,)))
        normed_ref[c] = normed
    for c in range(blocks):
        if c == 0 or c == half_up:
            copies[c // half_up].wait()
        up += dot(normed_ref[c], up_ref[c])
    affinity = jax.nn.sigmoid(logits)
    lane = iota((rows, experts), 1)
    mine = jnp.zeros((rows, 1), f32)
    whole = jnp.zeros((rows, 1), f32)
    for k in range(routes_ref.shape[1]):
        choice = routes_ref[:, k : k + 1]
        picked = jnp.sum(jnp.where(lane == choice, affinity, 0.0), axis=1, keepdims=True)
        whole += picked
        mine += jnp.where(choice == me[0], picked, 0.0)
    weight = route_scale * mine / whole
    copies[2].wait()
    copies[3].wait()
    active = (gate / (1.0 + jnp.exp(-gate)) * up).astype(bf16)
    for c in range(blocks):
        got = dot(active, down_ref[:, c * cols : (c + 1) * cols])
        each = out_ref.shape[0] // blocks
        got = (got * weight).reshape(each, rows // each, cols)
        out_ref[c * each : (c + 1) * each] = got.astype(bf16)


def experts_here(shape, hidden, gain, router, routes, me, gate, up, down):
    vmem = pl.BlockSpec(memory_space=pltpu.VMEM)
    return pl.pallas_call(
        expert_kernel,
        out_shape=jax.ShapeDtypeStruct(shape, bf16),
        in_specs=[pl.BlockSpec(memory_space=pltpu.SMEM)]
        + [vmem] * 5
        + [pl.BlockSpec(memory_space=pltpu.HBM)] * 2,
        out_specs=vmem,
        scratch_shapes=[
            pltpu.VMEM(up.shape, bf16),
            pltpu.VMEM(down.shape, bf16),
            pltpu.VMEM(hidden.shape, bf16),
            pltpu.SemaphoreType.DMA((4,)),
        ],
        compiler_params=pltpu.CompilerParams(vmem_limit_bytes=VMEM_LIMIT),
        name="experts",
    )(me, hidden, gain, router, routes, gate, in_hbm(up), in_hbm(down))


def on_device(
    queries,
    latent_cache,
    context_lengths,
    value_up,
    out_proj,
    residual,
    norm_gain,
    router,
    routes,
    expert_gate,
    expert_up,
    expert_down,
):
    reqs, pair, heads, depth = queries.shape
    lat, vdim = value_up.shape[1:]
    scale = 1.0 / math.sqrt(vdim + depth - lat)
    n_ctx, n_exp = lax.axis_size("ctx"), lax.axis_size("exp")
    n_all = n_ctx * n_exp
    everyone = ("ctx", "exp")
    ctx, exp = lax.axis_index("ctx"), lax.axis_index("exp")
    own_rows, model = residual.shape
    top = routes.shape[1]
    cols = model // n_ctx
    experts = router.shape[1]

    def swap(x, axes):
        return lax.all_to_all(x, axes, split_axis=0, concat_axis=0, tiled=True)

    def spread(x, axes, size):
        return swap(jnp.broadcast_to(x[None], (size, *x.shape)), axes)

    early = reqs * 5 // 16
    counts = (early, reqs - early)
    per = pair * heads
    q = queries.reshape(reqs * per, depth)
    late = spread(q[early * per :], "exp", n_exp)
    late = late.reshape(n_exp, counts[1], per, depth).transpose(1, 0, 2, 3).reshape(counts[1], n_exp * per, depth)
    q, late = lax.optimization_barrier((q[: early * per], late))
    late = lax.all_gather(late, "ctx", axis=0)
    q = spread(q, "ctx", n_ctx)
    q = q.reshape(n_ctx, early, per, depth).transpose(1, 0, 2, 3).reshape(early * n_ctx * per, depth)
    q = spread(q, "exp", n_exp).reshape(n_exp, early, n_ctx * per, depth)

    base = ((ctx * n_exp + exp) * latent_cache.shape[1]).reshape(1)
    routes_row = jnp.zeros((1, LANES), f32).at[0, : own_rows * top].set(routes.reshape(-1).astype(f32))
    cache = in_hbm(latent_cache.swapaxes(1, 2))
    rest = (cache, context_lengths, base, routes_row, scale, n_ctx, n_exp, lat)
    sent = attend(q, *rest, 0, False)
    up, late = lax.optimization_barrier((value_up, late))
    all_up = lax.all_gather(up, "ctx", axis=0)
    late = in_hbm(late)
    arrived = swap(sent, "exp")
    sent, arrived = lax.optimization_barrier((attend(late, *rest, early, True), arrived))
    sums, stats, route_rows = merge_early(arrived, early, lat)
    all_routes = route_rows[:, : own_rows * top].astype(jnp.int32).reshape(n_exp, own_rows, top)
    sent, sums = lax.optimization_barrier((sent, sums))
    arrived = swap(sent, "exp")
    arrived = swap(merge_late(sums, stats, arrived, all_up, reqs - early), "ctx")
    own = lax.dynamic_slice_in_dim(residual, ctx * cols, cols, 1).astype(f32)
    arrived, own = lax.optimization_barrier((arrived, own))
    terms = project(arrived, ctx.reshape(1), out_proj, n_ctx, n_exp)

    terms = swap(terms, everyone)
    attention = jnp.sum(terms.astype(f32), axis=0)
    hidden = (own + attention).astype(bf16)

    slots = max(2, own_rows * top // experts)
    before = jnp.tril(jnp.ones((own_rows, own_rows), jnp.int32), -1)

    def slot_of(named, axis):
        shape = (1,) * axis + (own_rows, own_rows) + (1,) * (named.ndim - 1 - axis)
        earlier = jnp.sum(before.reshape(shape) * jnp.expand_dims(named, axis), axis=axis + 1)
        return jnp.where(named == 1, earlier, -1)

    named = jnp.sum((routes[:, :, None] == jnp.arange(experts)).astype(jnp.int32), axis=1)
    place = (slot_of(named, 0)[:, :, None] == jnp.arange(slots)).astype(bf16)
    place = jnp.broadcast_to(place[:, None], (own_rows, n_ctx, experts, slots)).reshape(own_rows, -1)
    rows = dot(place, hidden, ((0,), (0,))).astype(bf16)
    rows = swap(rows.reshape(n_all, slots, cols), everyone)

    named = jnp.any(all_routes == exp, axis=2).astype(jnp.int32)
    taken = (slot_of(named, 1)[:, None, :] == jnp.arange(slots)[None, :, None]).astype(jnp.int32)
    slot_routes = jnp.sum(taken[..., None] * all_routes[:, None], axis=2).reshape(n_exp * slots, top)
    mixed = experts_here(
        (n_all, slots, cols),
        rows.reshape(n_ctx, n_exp * slots, cols),
        norm_gain.reshape(n_ctx, 1, cols),
        router.T.reshape(experts, n_ctx, cols).transpose(1, 0, 2),
        slot_routes,
        exp.reshape(1),
        expert_gate.reshape(n_ctx, cols, -1),
        expert_up.reshape(n_ctx, cols, -1),
        expert_down[0],
    )
    mixed = swap(mixed, everyone)
    mixture = dot(place, mixed.reshape(n_all * slots, cols))
    return (hidden.astype(f32) + mixture).astype(bf16)


def solution(mesh):
    return jax.shard_map(
        on_device,
        mesh=mesh,
        in_specs=(
            P("req", None, ("ctx", "exp"), None),
            P("req", ("ctx", "exp"), None),
            P("req"),
            P(("ctx", "exp"), None, None),
            P(("ctx", "exp"), None),
            P(("req", "exp"), None),
            P(),
            P(),
            P(("req", "exp"), None),
            P("exp", None, "ctx"),
            P("exp", None, "ctx"),
            P("exp", "ctx", None),
        ),
        out_specs=P(("req", "exp"), "ctx"),
        check_vma=False,
    )
```
